32 devices in a mesh: region: 2 (over y), cell: 8 (over z, x), ray: 2 (over core).
Axes of the slice: x: 2, y: 2, z: 4, core: 2. Of those that a mesh axis runs over, the one named last changes fastest.
Arguments:
- blocks: bfloat16 [16, 2, 96, 128, 128], P(('region', 'cell'), 'ray'), parts along dimension 0, may hold values from -0.109375 to 0.109375
- row_ids: int32 [16, 2, 96], P(('region', 'cell'), 'ray'), parts along dimension 0, may hold values from 0 to 31
- col_ids: int32 [16, 2, 96], P(('region', 'cell'), 'ray'), parts along dimension 0, may hold values from 0 to 15
- counts: int32 [16, 2], P(('region', 'cell'), 'ray'), parts along dimension 0, may hold values from 48 to 96, as said below
- ray_weight: float32 [16384], P(('region', 'ray')), parts along dimension 0, may hold values from 0.25 to 4
- probes: float32 [16, 32, 1024], P(None, ('region', 'cell')), parts along dimension 1, may hold values from -6 to 6
- stiffness: float32 [32, 1024], P(('region', 'cell')), parts along dimension 0, may hold values from 0.05 to 0.5
Outputs:
- applied: float32 [16, 32, 1024], P(None, ('region', 'cell')), parts along dimension 1
- diag_estimate: float32 [32, 1024], P(('region', 'cell')), parts along dimension 0
The draws below stay inside these ranges and needn't reach their ends.
There are 2 independent parts, one for each index of `region`. The reference program is written for one: setup_inputs(seed, part) draws one part's arguments, and reference() takes and returns one part's arrays. A program takes and returns all parts, laid end to end along the dimension named above; each array names one. Nothing has to cross between parts.
Inputs may be any that keep to these rules, and one draw needn't show every extreme that they name: `counts`: some device holds exactly 96 live slots in every draw.
All inputs are finite; a program needn't handle non-finite values.
Results may differ from the reference program's by a relative error of at most 0.0055.
Values may be sent and summed in bfloat16 or wider, within the bound.
No kernel may reach another device: no remote copies, remote signals or barrier semaphores. Data moves between devices by JAX's collectives and lax.ppermute only.
A program may use at most 64 MiB of HBM per device.

```python
import math
import jax
import jax.numpy as jnp
from jax import lax

PROBES = 16
BLOCK = 128
NY = 32
NZ = 32
RB_R = 32
NB_DEV = 96
NX = 16
CB_DEV = 16
RAYS = 8192
N_CELL = 8
N_RAY = 2


def draw_counts(key, part):
    key = jax.random.fold_in(key, 7)
    first, second = jax.random.split(key)
    values = jax.random.randint(first, (N_CELL * N_RAY,), NB_DEV // 2, NB_DEV + 1)
    place = jax.random.randint(second, (), 0, N_CELL * N_RAY)
    values = values.at[place].set(NB_DEV)
    return values.reshape(N_CELL, N_RAY).astype(jnp.int32)


def with_ends(values, rng, low, high):
    index_at = [jax.random.randint(jax.random.fold_in(rng, axis), (), 0, length) for axis, length in enumerate(values.shape)]
    widest = values.shape.index(max(values.shape))
    beside = index_at[:widest] + [(index_at[widest] + 1) % values.shape[widest]] + index_at[widest + 1:]
    return values.at[tuple(index_at)].set(low).at[tuple(beside)].set(high)


def steps_of(rng, shape, cuts, smallest, largest):
    gain = 1.0
    for position, shards_of in cuts:
        draws = jax.random.uniform(jax.random.fold_in(jax.random.fold_in(rng, 6), position), (shards_of,), jnp.float32, smallest / len(cuts), largest / len(cuts))
        gain = gain * jnp.repeat(jnp.exp(draws), shape[position] // shards_of).reshape((-1,) + (1,) * (len(shape) - 1 - position))
    return gain


def scatter_about(own_key, dims, width, bound, cuts=(), kind=jnp.bfloat16):
    level = steps_of(own_key, dims, cuts, -0.22, 0.18) if cuts else 1.0
    array = jax.random.normal(own_key, dims, jnp.float32) * width * level
    return jnp.minimum(jnp.maximum(array, -bound), bound).astype(kind)


def setup_inputs(seed: int = 0, part: int = 0) -> dict:
    key_list = jax.random.split(jax.random.key(seed), 8)
    part_keys = jax.random.split(jax.random.fold_in(key_list[7], part), 8)
    blocks = scatter_about(part_keys[0], (N_CELL, N_RAY, NB_DEV, BLOCK, BLOCK), (BLOCK * NB_DEV * N_CELL // RB_R) ** -0.5, 0.109375, ((0, 8), (1, 2)))
    row_ids = with_ends(jax.random.randint(part_keys[1], (N_CELL, N_RAY, NB_DEV), 0, RB_R), jax.random.fold_in(part_keys[1], 1), 0, RB_R - 1).astype(jnp.int32)
    col_ids = with_ends(jax.random.randint(part_keys[2], (N_CELL, N_RAY, NB_DEV), 0, CB_DEV), jax.random.fold_in(part_keys[2], 1), 0, CB_DEV - 1).astype(jnp.int32)
    counts = draw_counts(jax.random.fold_in(jax.random.fold_in(key_list[7], part), 71), part)
    ray_weight = jnp.clip(jnp.exp(math.log(4.0) - 2.7725887 * jax.random.uniform(part_keys[4], (RAYS,), jnp.float32) ** steps_of(part_keys[4], (RAYS,), ((0, 2),), -0.2, 0.2)), 0.25, 4.0)
    probes = scatter_about(part_keys[5], (PROBES, NX, NY * NZ), 1.0, 6.0, ((1, 8),), jnp.float32)
    stiffness = jnp.clip(jnp.exp(math.log(0.5) - 2.3025851 * jax.random.uniform(part_keys[6], (NX, NY * NZ), jnp.float32) ** steps_of(part_keys[6], (NX, NY * NZ), ((0, 8),), -0.2, 0.2)), 0.05, 0.5)
    return {"blocks": blocks, "row_ids": row_ids, "col_ids": col_ids, "counts": counts, "ray_weight": ray_weight, "probes": probes, "stiffness": stiffness}


def smoothing(padded_probe, padded_stiff):
    center = padded_probe[:, 1:-1, 1:-1, 1:-1]
    center_s = padded_stiff[1:-1, 1:-1, 1:-1]
    total = jnp.zeros_like(center)
    moves = [(0, 1), (0, -1), (1, 1), (1, -1), (2, 1), (2, -1)]
    for axis_pick, step in moves:
        starts = [1, 1, 1]
        starts[axis_pick] = 1 + step
        ends = [padded_stiff.shape[0] - 2 + starts[0], padded_stiff.shape[1] - 2 + starts[1], padded_stiff.shape[2] - 2 + starts[2]]
        near_p = padded_probe[:, starts[0]:ends[0], starts[1]:ends[1], starts[2]:ends[2]]
        near_s = padded_stiff[starts[0]:ends[0], starts[1]:ends[1], starts[2]:ends[2]]
        total = total + 0.5 * (center_s + near_s)[None] * (center - near_p)
    return total


def reference(blocks, row_ids, col_ids, counts, ray_weight, probes, stiffness):
    flat = probes.astype(jnp.bfloat16).reshape(PROBES, N_CELL, CB_DEV, BLOCK)
    slot_ix = jnp.arange(NB_DEV, dtype=jnp.int32)
    row_range = jnp.arange(RB_R, dtype=jnp.int32)
    col_range = jnp.arange(CB_DEV, dtype=jnp.int32)
    ray_pick = jnp.arange(N_RAY, dtype=jnp.int32)[:, None]

    def forward(carry, cell_ix):
        tiles = blocks[cell_ix].astype(jnp.float32)
        rows = row_ids[cell_ix]
        cols = col_ids[cell_ix]
        live = (slot_ix[None, :] < counts[cell_ix][:, None]).astype(jnp.float32)
        picked = jnp.take(flat[:, cell_ix], cols, axis=1).astype(jnp.float32)
        prod = jnp.einsum('pwnc,wnrc->pwnr', picked, tiles) * live[None, :, :, None]
        hot = (rows[..., None] == row_range).astype(jnp.float32)
        return carry + jnp.einsum('pwnr,wnk->pwkr', prod, hot, precision=lax.Precision.HIGHEST), None

    start = jnp.zeros((PROBES, N_RAY, RB_R, BLOCK), jnp.float32)
    ray_sum, unused = lax.scan(forward, start, jnp.arange(N_CELL, dtype=jnp.int32))
    weighted = (ray_sum * ray_weight.reshape(N_RAY, RB_R, BLOCK)[None]).astype(jnp.bfloat16)

    def backward(carry, cell_ix):
        tiles = blocks[cell_ix].astype(jnp.float32)
        rows = row_ids[cell_ix]
        cols = col_ids[cell_ix]
        live = (slot_ix[None, :] < counts[cell_ix][:, None]).astype(jnp.float32)
        picked = weighted[:, ray_pick, rows].astype(jnp.float32)
        prod = jnp.einsum('pwnr,wnrc->pwnc', picked, tiles) * live[None, :, :, None]
        hot = (cols[..., None] == col_range).astype(jnp.float32)
        return carry, jnp.einsum('pwnc,wnk->pkc', prod, hot, precision=lax.Precision.HIGHEST)

    unused2, pieces = lax.scan(backward, jnp.float32(0.0), jnp.arange(N_CELL, dtype=jnp.int32))
    data_term = jnp.transpose(pieces, (1, 0, 2, 3)).reshape(PROBES, NX, NY * NZ)
    grid_p = probes.reshape(PROBES, NX, NY, NZ)
    grid_s = stiffness.reshape(NX, NY, NZ)
    padded_probe = jnp.pad(grid_p, ((0, 0), (1, 1), (1, 1), (1, 1)))
    padded_stiff = jnp.pad(grid_s, ((1, 1), (1, 1), (1, 1)))
    smooth_term = smoothing(padded_probe, padded_stiff).reshape(PROBES, NX, NY * NZ)
    applied = data_term + smooth_term
    diag_estimate = jnp.mean(probes * applied, axis=0)
    return applied, diag_estimate
```

```python
import jax
import jax.numpy as jnp
from jax import lax
from jax.experimental import pallas as pl
from jax.experimental.pallas import tpu as pltpu
from jax.sharding import PartitionSpec as P

NY = 32
NZ = 32
CHUNK = 12
F32 = jnp.float32
BF16 = jnp.bfloat16
VMEM = pl.BlockSpec(memory_space=pltpu.VMEM)
SMEM = pl.BlockSpec(memory_space=pltpu.SMEM)
ANY = pl.BlockSpec(memory_space=pl.ANY)


def pieces(slots):
    return [(i, min(CHUNK, slots - i)) for i in range(0, slots, CHUNK)]


def block_copies(blocks, tiles, sems):
    slots = tiles.shape[0]
    return [
        pltpu.make_async_copy(
            blocks.at[0, 0, pl.ds(start, size)],
            tiles.at[pl.ds(start, size)],
            sems.at[i],
        )
        for i, (start, size) in enumerate(pieces(slots))
    ]


def forward_kernel(
    counts, rows, cols, blocks, probes, stiff, total, sent, low, high, flat, tiles, acc, flat16, sems
):
    slots, width = tiles.shape[0], tiles.shape[1]
    nprobe, slabs, plane = probes.shape
    each = plane // width
    nrows = total.shape[0]
    copies = block_copies(blocks, tiles, sems)
    for copy in copies:
        copy.start()
    for s in range(slabs):
        for j in range(each):
            value = probes[:, s, j * width : (j + 1) * width]
            flat[s * each + j] = value
            flat16[s * each + j] = value.astype(BF16)
    for out, s in ((low, 0), (high, slabs - 1)):
        out[0:each] = flat16[s * each : (s + 1) * each]
        out[each] = jnp.zeros((nprobe, width), BF16)
        for j in range(each):
            out[each, j : j + 1, :] = stiff[s : s + 1, j * width : (j + 1) * width].astype(BF16)
    acc[...] = jnp.zeros_like(acc)
    live = counts[0, 0]
    for copy, (start, size) in zip(copies, pieces(slots)):
        copy.wait()
        for n in range(start, start + size):
            row = jnp.where(n < live, rows[0, 0, n], nrows)
            acc[row] += lax.dot_general(
                flat16[cols[0, 0, n]],
                tiles[n],
                (((1,), (1,)), ((), ())),
                preferred_element_type=F32,
            )
    value = acc[0:nrows]
    total[...] = value
    sent[...] = value.astype(BF16)


def backward_kernel(counts, rows, cols, blocks, weighted, part, tiles, acc, sems):
    slots = tiles.shape[0]
    ncols = part.shape[0]
    copies = block_copies(blocks, tiles, sems)
    for copy in copies:
        copy.start()
    acc[...] = jnp.zeros_like(acc)
    live = counts[0, 0]
    for copy, (start, size) in zip(copies, pieces(slots)):
        copy.wait()
        for n in range(start, start + size):
            col = jnp.where(n < live, cols[0, 0, n], ncols)
            acc[col] += jnp.dot(weighted[rows[0, 0, n]], tiles[n], preferred_element_type=F32)
    part[...] = acc[0:ncols].astype(BF16)


def smooth_kernel(flat, stiff, below, above, smooth):
    ncols, nprobe, width = flat.shape
    slabs = stiff.shape[0]
    each = ncols // slabs
    lane = lax.broadcasted_iota(jnp.int32, (1, width), 1)
    at_z = lane % NZ

    def stiff_at(s, j):
        if j < 0 or j >= each:
            return jnp.zeros((1, width), F32)
        if s < 0:
            return below[each, j : j + 1, :].astype(F32)
        if s >= slabs:
            return above[each, j : j + 1, :].astype(F32)
        return stiff[s : s + 1, j * width : (j + 1) * width]

    def probe_at(s, j):
        if j < 0 or j >= each:
            return jnp.zeros((nprobe, width), F32)
        if s < 0:
            return below[j].astype(F32)
        if s >= slabs:
            return above[j].astype(F32)
        return flat[s * each + j]

    def neighbours(at, s, j):
        here, before, after = at(s, j), at(s, j - 1), at(s, j + 1)
        up = lambda v, by: pltpu.roll(v, width - by, 1)
        down = lambda v, by: pltpu.roll(v, by, 1)
        return [
            at(s + 1, j),
            at(s - 1, j),
            jnp.where(lane < width - NZ, up(here, NZ), up(after, NZ)),
            jnp.where(lane >= NZ, down(here, NZ), down(before, NZ)),
            jnp.where(at_z < NZ - 1, up(here, 1), 0.0),
            jnp.where(at_z > 0, down(here, 1), 0.0),
        ]

    for s in range(slabs):
        for j in range(each):
            here_s, here_p = stiff_at(s, j), probe_at(s, j)
            term = jnp.zeros((nprobe, width), F32)
            for near_s, near_p in zip(neighbours(stiff_at, s, j), neighbours(probe_at, s, j)):
                term = term + 0.5 * (here_s + near_s) * (here_p - near_p)
            smooth[s * each + j] = term


def combine_kernel(flat, smooth, mine, other, applied, diag):
    ncols, nprobe, width = flat.shape
    slabs = applied.shape[1]
    each = ncols // slabs
    for s in range(slabs):
        for j in range(each):
            c = s * each + j
            data = mine[c].astype(F32) + other[c].astype(F32)
            value = data + smooth[c]
            applied[:, s, j * width : (j + 1) * width] = value
            diag[s : s + 1, j * width : (j + 1) * width] = jnp.mean(
                flat[c] * value, axis=0, keepdims=True
            )


def power_of_two(n):
    return n & (n - 1) == 0


def local(blocks, row_ids, col_ids, counts, ray_weight, probes, stiffness):
    slots, width = blocks.shape[2], blocks.shape[3]
    nprobe, slabs, plane = probes.shape
    ncols = slabs * plane // width
    nrows = ray_weight.shape[0] // width
    each = plane // width
    ncopies = len(pieces(slots))
    ncell, nray = lax.axis_size("cell"), lax.axis_size("ray")
    shape = jax.ShapeDtypeStruct
    params = pltpu.CompilerParams(vmem_limit_bytes=16 * 1024 * 1024)
    flops = 2 * slots * nprobe * width * width

    total, sent, low, high, flat = pl.pallas_call(
        forward_kernel,
        out_shape=(
            shape((nrows, nprobe, width), F32),
            shape((nrows, nprobe, width), BF16),
            shape((each + 1, nprobe, width), BF16),
            shape((each + 1, nprobe, width), BF16),
            shape((ncols, nprobe, width), F32),
        ),
        in_specs=[SMEM, SMEM, SMEM, ANY, VMEM, VMEM],
        out_specs=(VMEM,) * 5,
        scratch_shapes=[
            pltpu.VMEM((slots, width, width), BF16),
            pltpu.VMEM((nrows + 1, nprobe, width), F32),
            pltpu.VMEM((ncols, nprobe, width), BF16),
            pltpu.SemaphoreType.DMA((ncopies,)),
        ],
        compiler_params=params,
        cost_estimate=pl.CostEstimate(flops=flops, bytes_accessed=2 * slots * width * width, transcendentals=0),
        name="forward",
    )(counts, row_ids, col_ids, blocks, probes, stiffness)

    up = [(i, i + 1) for i in range(ncell - 1)]
    below = lax.ppermute(high, "cell", up)
    above = lax.ppermute(low, "cell", [(j, i) for i, j in up])

    if power_of_two(ncell):
        step = 1
        while step < ncell:
            got = lax.ppermute(sent, "cell", [(i, i ^ step) for i in range(ncell)])
            total = total + got.astype(F32)
            sent = total.astype(BF16)
            step *= 2
    else:
        total = lax.psum(total, "cell")
    weighted = (total * ray_weight.reshape(nrows, 1, width)).astype(BF16)

    part = pl.pallas_call(
        backward_kernel,
        out_shape=shape((ncols, nprobe, width), BF16),
        in_specs=[SMEM, SMEM, SMEM, ANY, VMEM],
        out_specs=VMEM,
        scratch_shapes=[
            pltpu.VMEM((slots, width, width), BF16),
            pltpu.VMEM((ncols + 1, nprobe, width), F32),
            pltpu.SemaphoreType.DMA((ncopies,)),
        ],
        compiler_params=params,
        cost_estimate=pl.CostEstimate(flops=flops, bytes_accessed=2 * slots * width * width, transcendentals=0),
        name="backward",
    )(counts, row_ids, col_ids, blocks, weighted)

    if nray == 2:
        other = lax.ppermute(part, "ray", [(0, 1), (1, 0)])
    else:
        other = lax.psum(part.astype(F32), "ray").astype(F32) - part.astype(F32)

    smooth = pl.pallas_call(
        smooth_kernel,
        out_shape=shape((ncols, nprobe, width), F32),
        in_specs=[VMEM] * 4,
        out_specs=VMEM,
        compiler_params=params,
        name="smooth",
    )(flat, stiffness, below, above)

    return pl.pallas_call(
        combine_kernel,
        out_shape=(shape((nprobe, slabs, plane), F32), shape((slabs, plane), F32)),
        in_specs=[VMEM] * 4,
        out_specs=(VMEM, VMEM),
        compiler_params=params,
        name="combine",
    )(flat, smooth, part, other)


def solution(mesh):
    return jax.shard_map(
        local,
        mesh=mesh,
        in_specs=(
            P(("region", "cell"), "ray", None, None, None),
            P(("region", "cell"), "ray", None),
            P(("region", "cell"), "ray", None),
            P(("region", "cell"), "ray"),
            P(("region", "ray")),
            P(None, ("region", "cell"), None),
            P(("region", "cell"), None),
        ),
        out_specs=(P(None, ("region", "cell"), None), P(("region", "cell"), None)),
        check_vma=False,
    )
```

```python
import jax
import jax.numpy as jnp
from jax import lax
from jax.experimental import pallas as pl
from jax.experimental.pallas import tpu as pltpu
from jax.sharding import PartitionSpec as P

NZ = 32
CHUNKS = 2
F32 = jnp.float32
BF16 = jnp.bfloat16
I32 = jnp.int32
VMEM = pl.BlockSpec(memory_space=pltpu.VMEM)
SMEM = pl.BlockSpec(memory_space=pltpu.SMEM)
HBM = pl.BlockSpec(memory_space=pltpu.HBM)


def groups(start, size):
    return [tuple(range(n, min(n + 2, start + size))) for n in range(start, start + size, 2)]


def forward_kernel(
    counts, rows_in, cols_in, blocks, probes_in, stiff_in,
    tiles, total, sent, odd, flat, stiff, rows, cols,
    probes, acc, flat16, sems, small,
):
    slots, width = tiles.shape[0], tiles.shape[1]
    nprobe, slabs, plane = probes.shape
    each = plane // width
    nrows = total.shape[0]
    run = -(-slots // CHUNKS)
    runs = [(i, min(run, slots - i)) for i in range(0, slots, run)]
    pairs = [(probes_in, probes), (cols_in, cols), (rows_in, rows), (stiff_in, stiff)]
    first = [pltpu.make_async_copy(a, b, small.at[i]) for i, (a, b) in enumerate(pairs)]
    copies = [
        pltpu.make_async_copy(blocks.at[0, 0, pl.ds(s, z)], tiles.at[pl.ds(s, z)], sems.at[i])
        for i, (s, z) in enumerate(runs)
    ]
    for copy in first + copies:
        copy.start()
    acc[...] = jnp.zeros_like(acc)
    for copy in first:
        copy.wait()
    for s in range(slabs):
        for j in range(each):
            value = probes[:, s, j * width : (j + 1) * width]
            flat[s * each + j] = value
            flat16[s * each + j] = value.astype(BF16)
    even = lax.rem(lax.axis_index("cell"), 2) == 0
    top = (slabs - 1) * each
    for j in range(each):
        low, high = flat16[j], flat16[top + j]
        sent[nrows + j] = jnp.where(even, high, low)
        odd[j] = jnp.where(even, low, high)
    sent[nrows + each] = jnp.zeros((nprobe, width), BF16)
    odd[each] = jnp.zeros((nprobe, width), BF16)
    for j in range(each):
        low = stiff[0:1, j * width : (j + 1) * width].astype(BF16)
        high = stiff[slabs - 1 : slabs, j * width : (j + 1) * width].astype(BF16)
        sent[nrows + each, j : j + 1, :] = jnp.where(even, high, low)
        odd[each, j : j + 1, :] = jnp.where(even, low, high)
    live = counts[0, 0]
    for copy, (start, size) in zip(copies, runs):
        copy.wait()
        outs = []
        for group in groups(start, size):
            left = jnp.concatenate([flat16[cols[0, 0, n]] for n in group], axis=0)
            right = jnp.concatenate([tiles[n] for n in group], axis=0)
            out = lax.dot_general(left, right, (((1,), (1,)), ((), ())), preferred_element_type=F32)
            outs += [
                (n, out[i * nprobe : (i + 1) * nprobe, i * width : (i + 1) * width])
                for i, n in enumerate(group)
            ]
        for n, out in outs:
            acc[jnp.where(n < live, rows[0, 0, n], nrows)] += out
    value = acc[0:nrows]
    total[...] = value
    sent[0:nrows] = value.astype(BF16)


def backward_kernel(counts, rows, cols, tiles, total, got, weight, part, weighted, acc):
    slots, width = tiles.shape[0], tiles.shape[1]
    nrows, nprobe = total.shape[0], total.shape[1]
    ncols = part.shape[0]
    for k in range(nrows):
        value = total[k] + got[k].astype(F32)
        weighted[k] = (value * weight[k : k + 1, :]).astype(BF16)
    acc[...] = jnp.zeros_like(acc)
    live = counts[0, 0]
    outs = []
    for group in groups(0, slots):
        left = jnp.concatenate([weighted[rows[0, 0, n]] for n in group], axis=0)
        right = jnp.concatenate([tiles[n] for n in group], axis=1)
        out = jnp.dot(left, right, preferred_element_type=F32)
        outs += [
            (n, out[i * nprobe : (i + 1) * nprobe, i * width : (i + 1) * width])
            for i, n in enumerate(group)
        ]
    for n, out in outs:
        acc[jnp.where(n < live, cols[0, 0, n], ncols)] += out
    part[...] = acc[0:ncols].astype(BF16)


def smooth_kernel(flat, stiff, got, odd, smooth, below, above):
    ncols, nprobe, width = flat.shape
    slabs = stiff.shape[0]
    each = ncols // slabs
    nrows = got.shape[0] - each - 1
    lane = lax.broadcasted_iota(I32, (1, width), 1)
    at_z = lane % NZ
    even = lax.rem(lax.axis_index("cell"), 2) == 0
    for j in range(each + 1):
        pair, other = got[nrows + j], odd[j]
        below[j] = jnp.where(even, other, pair).astype(F32)
        above[j] = jnp.where(even, pair, other).astype(F32)

    def stiff_at(s, j):
        if j < 0 or j >= each:
            return jnp.zeros((1, width), F32)
        if s < 0:
            return below[each, j : j + 1, :]
        if s >= slabs:
            return above[each, j : j + 1, :]
        return stiff[s : s + 1, j * width : (j + 1) * width]

    def probe_at(s, j):
        if j < 0 or j >= each:
            return jnp.zeros((nprobe, width), F32)
        if s < 0:
            return below[j]
        if s >= slabs:
            return above[j]
        return flat[s * each + j]

    def up(value, by):
        return pltpu.roll(value, width - by, 1)

    def down(value, by):
        return pltpu.roll(value, by, 1)

    def neighbours(at, s, j):
        here, before, after = at(s, j), at(s, j - 1), at(s, j + 1)
        return [
            at(s + 1, j),
            at(s - 1, j),
            jnp.where(lane < width - NZ, up(here, NZ), up(after, NZ)),
            jnp.where(lane >= NZ, down(here, NZ), down(before, NZ)),
            jnp.where(at_z < NZ - 1, up(here, 1), 0.0),
            jnp.where(at_z > 0, down(here, 1), 0.0),
        ]

    for s in range(slabs):
        for j in range(each):
            here_s, here_p = stiff_at(s, j), probe_at(s, j)
            term = jnp.zeros((nprobe, width), F32)
            for near_s, near_p in zip(neighbours(stiff_at, s, j), neighbours(probe_at, s, j)):
                term = term + 0.5 * (here_s + near_s) * (here_p - near_p)
            smooth[s * each + j] = term


def combine_kernel(flat, smooth, mine, other, applied, diag):
    ncols, nprobe, width = flat.shape
    slabs = applied.shape[1]
    each = ncols // slabs
    for s in range(slabs):
        for j in range(each):
            c = s * each + j
            value = mine[c].astype(F32) + other[c].astype(F32) + smooth[c]
            applied[:, s, j * width : (j + 1) * width] = value
            diag[s : s + 1, j * width : (j + 1) * width] = jnp.mean(
                flat[c] * value, axis=0, keepdims=True
            )


def local(blocks, row_ids, col_ids, counts, ray_weight, probes, stiffness):
    slots, width = blocks.shape[2], blocks.shape[3]
    nprobe, slabs, plane = probes.shape
    ncols = slabs * plane // width
    nrows = ray_weight.shape[0] // width
    each = plane // width
    ncell, nray = lax.axis_size("cell"), lax.axis_size("ray")
    assert ncell > 1 and ncell & (ncell - 1) == 0 and nray == 2
    params = pltpu.CompilerParams(vmem_limit_bytes=8 * 1024 * 1024)
    cost = pl.CostEstimate(
        flops=2 * slots * nprobe * width * width,
        bytes_accessed=2 * slots * width * width,
        transcendentals=0,
    )
    pinned = [
        pltpu.with_memory_space_constraint(x, pltpu.HBM)
        for x in (row_ids, col_ids, blocks, probes, stiffness)
    ]
    tiles, total, sent, odd, flat, stiff, rows, cols = pl.pallas_call(
        forward_kernel,
        out_shape=(
            pltpu.VMEM((slots, width, width), BF16),
            pltpu.VMEM((nrows, nprobe, width), F32),
            pltpu.VMEM((nrows + each + 1, nprobe, width), BF16),
            pltpu.VMEM((each + 1, nprobe, width), BF16),
            pltpu.VMEM((ncols, nprobe, width), F32),
            pltpu.VMEM((slabs, plane), F32),
            pltpu.SMEM(row_ids.shape, I32),
            pltpu.SMEM(col_ids.shape, I32),
        ),
        in_specs=[SMEM] + [HBM] * 5,
        out_specs=(VMEM,) * 6 + (SMEM,) * 2,
        scratch_shapes=[
            pltpu.VMEM((nprobe, slabs, plane), F32),
            pltpu.VMEM((nrows + 1, nprobe, width), F32),
            pltpu.VMEM((ncols, nprobe, width), BF16),
            pltpu.SemaphoreType.DMA((CHUNKS,)),
            pltpu.SemaphoreType.DMA((4,)),
        ],
        compiler_params=params,
        cost_estimate=cost,
        name="forward",
    )(counts, *pinned)

    above_odd = [(i, i + 1) for i in range(1, ncell - 1, 2)]
    across = lax.ppermute(odd, "cell", above_odd + [(j, i) for i, j in above_odd])

    step = 1
    while True:
        got = lax.ppermute(sent, "cell", [(i, i ^ step) for i in range(ncell)])
        if step == 1:
            halo = got
        step *= 2
        if step == ncell:
            break
        total = total + got[:nrows].astype(F32)
        sent = total.astype(BF16)
        if step == 4:
            total, sent, across = lax.optimization_barrier((total, sent, across))

    part = pl.pallas_call(
        backward_kernel,
        out_shape=pltpu.VMEM((ncols, nprobe, width), BF16),
        in_specs=[SMEM] * 3 + [VMEM] * 4,
        out_specs=VMEM,
        scratch_shapes=[
            pltpu.VMEM((nrows, nprobe, width), BF16),
            pltpu.VMEM((ncols + 1, nprobe, width), F32),
        ],
        compiler_params=params,
        cost_estimate=cost,
        name="backward",
    )(counts, rows, cols, tiles, total, got, ray_weight.reshape(nrows, width))

    other = lax.ppermute(part, "ray", [(0, 1), (1, 0)])

    smooth = pl.pallas_call(
        smooth_kernel,
        out_shape=pltpu.VMEM((ncols, nprobe, width), F32),
        in_specs=[VMEM] * 4,
        out_specs=VMEM,
        scratch_shapes=[pltpu.VMEM((each + 1, nprobe, width), F32)] * 2,
        compiler_params=params,
        name="smooth",
    )(flat, stiff, halo, across)

    return pl.pallas_call(
        combine_kernel,
        out_shape=(
            jax.ShapeDtypeStruct((nprobe, slabs, plane), F32),
            jax.ShapeDtypeStruct((slabs, plane), F32),
        ),
        in_specs=[VMEM] * 4,
        out_specs=(VMEM, VMEM),
        compiler_params=params,
        name="combine",
    )(flat, smooth, part, other)


def solution(mesh):
    return jax.shard_map(
        local,
        mesh=mesh,
        in_specs=(
            P(("region", "cell"), "ray", None, None, None),
            P(("region", "cell"), "ray", None),
            P(("region", "cell"), "ray", None),
            P(("region", "cell"), "ray"),
            P(("region", "ray")),
            P(None, ("region", "cell"), None),
            P(("region", "cell"), None),
        ),
        out_specs=(P(None, ("region", "cell"), None), P(("region", "cell"), None)),
        check_vma=False,
    )
```

```python
import jax
import jax.numpy as jnp
from jax import lax
from jax.experimental import pallas as pl
from jax.experimental.pallas import tpu as pltpu
from jax.sharding import PartitionSpec as P

NZ = 32
CHUNKS = 2
F32 = jnp.float32
BF16 = jnp.bfloat16
I32 = jnp.int32
VMEM = pl.BlockSpec(memory_space=pltpu.VMEM)
SMEM = pl.BlockSpec(memory_space=pltpu.SMEM)
HBM = pl.BlockSpec(memory_space=pltpu.HBM)


def groups(start, size):
    return [tuple(range(n, min(n + 2, start + size))) for n in range(start, start + size, 2)]


def looks_up():
    return lax.rem(lax.axis_index("cell") + lax.axis_index("ray"), 2) == 1


def forward_kernel(
    counts, rows_in, cols_in, blocks, probes_in, stiff_in,
    tiles, total, sent, edge, flat, stiff, rows, cols,
    probes, acc, flat16, sems, small,
):
    slots, width = tiles.shape[0], tiles.shape[1]
    nprobe, slabs, plane = probes.shape
    each = plane // width
    nrows = total.shape[0]
    run = -(-slots // CHUNKS)
    runs = [(i, min(run, slots - i)) for i in range(0, slots, run)]
    pairs = [(probes_in, probes), (cols_in, cols), (rows_in, rows), (stiff_in, stiff)]
    first = [pltpu.make_async_copy(a, b, small.at[i]) for i, (a, b) in enumerate(pairs)]
    copies = [
        pltpu.make_async_copy(blocks.at[0, 0, pl.ds(s, z)], tiles.at[pl.ds(s, z)], sems.at[i])
        for i, (s, z) in enumerate(runs)
    ]
    for copy in first + copies:
        copy.start()
    acc[...] = jnp.zeros_like(acc)
    for copy in first:
        copy.wait()
    for s in range(slabs):
        for j in range(each):
            value = probes[:, s, j * width : (j + 1) * width]
            flat[s * each + j] = value
            flat16[s * each + j] = value.astype(BF16)
    upper, top = looks_up(), (slabs - 1) * each
    for j in range(each):
        edge[j] = jnp.where(upper, flat16[top + j], flat16[j])
    edge[each] = jnp.zeros((nprobe, width), BF16)
    for j in range(each):
        low = stiff[0:1, j * width : (j + 1) * width]
        high = stiff[slabs - 1 : slabs, j * width : (j + 1) * width]
        edge[each, j : j + 1, :] = jnp.where(upper, high, low).astype(BF16)
    live = counts[0, 0]
    for copy, (start, size) in zip(copies, runs):
        copy.wait()
        outs = []
        for group in groups(start, size):
            left = jnp.concatenate([flat16[cols[0, 0, n]] for n in group], axis=0)
            right = jnp.concatenate([tiles[n] for n in group], axis=0)
            out = lax.dot_general(left, right, (((1,), (1,)), ((), ())), preferred_element_type=F32)
            outs += [
                (n, out[i * nprobe : (i + 1) * nprobe, i * width : (i + 1) * width])
                for i, n in enumerate(group)
            ]
        for n, out in outs:
            acc[jnp.where(n < live, rows[0, 0, n], nrows)] += out
    value = acc[0:nrows]
    total[...] = value
    sent[...] = value.astype(BF16)


def backward_kernel(
    counts, rows, cols, tiles, total, got, weight, flat, stiff, beyond, part, weighted, acc
):
    slots, width = tiles.shape[0], tiles.shape[1]
    nrows, nprobe = total.shape[0], total.shape[1]
    ncols = part.shape[0]
    for k in range(nrows):
        value = total[k] + got[k].astype(F32)
        weighted[k] = (value * weight[k : k + 1, :]).astype(BF16)
    acc[...] = jnp.zeros_like(acc)
    live = counts[0, 0]
    outs = []
    for group in groups(0, slots):
        left = jnp.concatenate([weighted[rows[0, 0, n]] for n in group], axis=0)
        right = jnp.concatenate([tiles[n] for n in group], axis=1)
        out = jnp.dot(left, right, preferred_element_type=F32)
        outs += [
            (n, out[i * nprobe : (i + 1) * nprobe, i * width : (i + 1) * width])
            for i, n in enumerate(group)
        ]
    for n, out in outs:
        acc[jnp.where(n < live, cols[0, 0, n], ncols)] += out
    slabs, plane = stiff.shape
    each = plane // width
    upper = looks_up()
    base = jnp.where(upper, (slabs - 1) * each, 0)
    for j in range(each):
        span = slice(j * width, (j + 1) * width)
        here = jnp.where(upper, stiff[slabs - 1 : slabs, span], stiff[0:1, span])
        scale = 0.5 * (here + beyond[each, j : j + 1, :].astype(F32))
        acc[base + j] += scale * (flat[base + j] - beyond[j].astype(F32))
    part[...] = acc[0:ncols].astype(BF16)


def smooth_kernel(flat, stiff, smooth):
    ncols, nprobe, width = flat.shape
    slabs = stiff.shape[0]
    each = ncols // slabs
    lane = lax.broadcasted_iota(I32, (1, width), 1)
    at_z = lane % NZ

    def stiff_at(s, j):
        if j < 0 or j >= each:
            return jnp.zeros((1, width), F32)
        return stiff[s : s + 1, j * width : (j + 1) * width]

    def probe_at(s, j):
        if j < 0 or j >= each:
            return jnp.zeros((nprobe, width), F32)
        return flat[s * each + j]

    def up(value, by):
        return pltpu.roll(value, width - by, 1)

    def down(value, by):
        return pltpu.roll(value, by, 1)

    def neighbours(at, s, j):
        here, before, after = at(s, j), at(s, j - 1), at(s, j + 1)
        return [at(t, j) for t in (s - 1, s + 1) if 0 <= t < slabs] + [
            jnp.where(lane < width - NZ, up(here, NZ), up(after, NZ)),
            jnp.where(lane >= NZ, down(here, NZ), down(before, NZ)),
            jnp.where(at_z < NZ - 1, up(here, 1), 0.0),
            jnp.where(at_z > 0, down(here, 1), 0.0),
        ]

    for s in range(slabs):
        for j in range(each):
            here_s, here_p = stiff_at(s, j), probe_at(s, j)
            term = jnp.zeros((nprobe, width), F32)
            for near_s, near_p in zip(neighbours(stiff_at, s, j), neighbours(probe_at, s, j)):
                term = term + 0.5 * (here_s + near_s) * (here_p - near_p)
            smooth[s * each + j] = term


def combine_kernel(flat, smooth, mine, other, applied, diag):
    ncols, nprobe, width = flat.shape
    slabs = applied.shape[1]
    each = ncols // slabs
    for s in range(slabs):
        for j in range(each):
            c = s * each + j
            value = mine[c].astype(F32) + other[c].astype(F32) + smooth[c]
            applied[:, s, j * width : (j + 1) * width] = value
            diag[s : s + 1, j * width : (j + 1) * width] = jnp.mean(
                flat[c] * value, axis=0, keepdims=True
            )


def local(blocks, row_ids, col_ids, counts, ray_weight, probes, stiffness):
    slots, width = blocks.shape[2], blocks.shape[3]
    nprobe, slabs, plane = probes.shape
    ncols = slabs * plane // width
    nrows = ray_weight.shape[0] // width
    each = plane // width
    ncell, nray = lax.axis_size("cell"), lax.axis_size("ray")
    assert ncell > 1 and ncell & (ncell - 1) == 0 and nray == 2
    params = pltpu.CompilerParams(vmem_limit_bytes=8 * 1024 * 1024)
    cost = pl.CostEstimate(
        flops=2 * slots * nprobe * width * width,
        bytes_accessed=2 * slots * width * width,
        transcendentals=0,
    )
    pinned = [
        pltpu.with_memory_space_constraint(x, pltpu.HBM)
        for x in (row_ids, col_ids, blocks, probes, stiffness)
    ]
    tiles, total, sent, edge, flat, stiff, rows, cols = pl.pallas_call(
        forward_kernel,
        out_shape=(
            pltpu.VMEM((slots, width, width), BF16),
            pltpu.VMEM((nrows, nprobe, width), F32),
            pltpu.VMEM((nrows, nprobe, width), BF16),
            pltpu.VMEM((each + 1, nprobe, width), BF16),
            pltpu.VMEM((ncols, nprobe, width), F32),
            pltpu.VMEM((slabs, plane), F32),
            pltpu.SMEM(row_ids.shape, I32),
            pltpu.SMEM(col_ids.shape, I32),
        ),
        in_specs=[SMEM] + [HBM] * 5,
        out_specs=(VMEM,) * 6 + (SMEM,) * 2,
        scratch_shapes=[
            pltpu.VMEM((nprobe, slabs, plane), F32),
            pltpu.VMEM((nrows + 1, nprobe, width), F32),
            pltpu.VMEM((ncols, nprobe, width), BF16),
            pltpu.SemaphoreType.DMA((CHUNKS,)),
            pltpu.SemaphoreType.DMA((4,)),
        ],
        compiler_params=params,
        cost_estimate=cost,
        name="forward",
    )(counts, *pinned)

    first = [(c, r) for c in range(ncell - 1) for r in range(nray) if (c + r) % 2 == 1]
    ends = [(c * nray + r, (c + 1) * nray + r) for c, r in first]
    beyond = lax.ppermute(edge, ("cell", "ray"), ends + [(j, i) for i, j in ends])

    steps = [1 << i for i in range(ncell.bit_length() - 1)]
    turns = list(zip(steps, steps[-1:] + steps[:-1]))
    for i, turn in enumerate(turns):
        pairs = [(c * nray + r, (c ^ turn[r]) * nray + r) for c in range(ncell) for r in range(nray)]
        got = lax.ppermute(sent, ("cell", "ray"), pairs)
        if i < len(turns) - 1:
            total = total + got.astype(F32)
            sent = total.astype(BF16)
    got, beyond = lax.optimization_barrier((got, beyond))

    part = pl.pallas_call(
        backward_kernel,
        out_shape=pltpu.VMEM((ncols, nprobe, width), BF16),
        in_specs=[SMEM] * 3 + [VMEM] * 7,
        out_specs=VMEM,
        scratch_shapes=[
            pltpu.VMEM((nrows, nprobe, width), BF16),
            pltpu.VMEM((ncols + 1, nprobe, width), F32),
        ],
        compiler_params=params,
        cost_estimate=cost,
        name="backward",
    )(counts, rows, cols, tiles, total, got, ray_weight.reshape(nrows, width), flat, stiff, beyond)

    other = lax.ppermute(part, "ray", [(0, 1), (1, 0)])

    smooth = pl.pallas_call(
        smooth_kernel,
        out_shape=pltpu.VMEM((ncols, nprobe, width), F32),
        in_specs=[VMEM] * 2,
        out_specs=VMEM,
        compiler_params=params,
        name="smooth",
    )(flat, stiff)

    return pl.pallas_call(
        combine_kernel,
        out_shape=(
            jax.ShapeDtypeStruct((nprobe, slabs, plane), F32),
            jax.ShapeDtypeStruct((slabs, plane), F32),
        ),
        in_specs=[VMEM] * 4,
        out_specs=(VMEM, VMEM),
        compiler_params=params,
        name="combine",
    )(flat, smooth, part, other)


def solution(mesh):
    return jax.shard_map(
        local,
        mesh=mesh,
        in_specs=(
            P(("region", "cell"), "ray", None, None, None),
            P(("region", "cell"), "ray", None),
            P(("region", "cell"), "ray", None),
            P(("region", "cell"), "ray"),
            P(("region", "ray")),
            P(None, ("region", "cell"), None),
            P(("region", "cell"), None),
        ),
        out_specs=(P(None, ("region", "cell"), None), P(("region", "cell"), None)),
        check_vma=False,
    )
```

```python
import jax
import jax.numpy as jnp
from jax import lax
from jax.experimental import pallas as pl
from jax.experimental.pallas import tpu as pltpu
from jax.sharding import PartitionSpec as P

NZ = 32
F32 = jnp.float32
BF16 = jnp.bfloat16
I32 = jnp.int32
VMEM = pl.BlockSpec(memory_space=pltpu.VMEM)
SMEM = pl.BlockSpec(memory_space=pltpu.SMEM)
HBM = pl.BlockSpec(memory_space=pltpu.HBM)


def rows_of(ref, s, j, slabs, ncols):
    return pl.ds(j * slabs + s, ref.shape[0] // ncols, stride=ncols)


def groups(slots):
    return [tuple(range(n, min(n + 2, slots))) for n in range(0, slots, 2)]


def even_cell():
    return lax.rem(lax.axis_index("cell"), 2) == 0


def prepare_kernel(
    rows_in, cols_in, probes_in, stiff_in, flat, paired, odd, probes, stiff, rows, cols, sems
):
    ncols, slabs = flat.shape[0], stiff.shape[0] // (paired.shape[0] - 1)
    each = ncols // slabs
    pairs = [(probes_in, probes), (stiff_in, stiff), (rows_in, rows), (cols_in, cols)]
    copies = [pltpu.make_async_copy(a, b, sems.at[i]) for i, (a, b) in enumerate(pairs)]
    for copy in copies:
        copy.start()
    for copy in copies:
        copy.wait()
    for s in range(slabs):
        for j in range(each):
            flat[s * each + j] = probes[rows_of(probes, s, j, slabs, ncols), :].astype(BF16)
    even, top = even_cell(), (slabs - 1) * each
    for out, high in ((paired, even), (odd, jnp.logical_not(even))):
        for j in range(each):
            out[j] = jnp.where(high, flat[top + j], flat[j])
        low_end = stiff[pl.ds(0, each, stride=slabs), :]
        high_end = stiff[pl.ds(slabs - 1, each, stride=slabs), :]
        end = jnp.where(high, high_end, low_end)
        rest = jnp.zeros((out.shape[1] - each, out.shape[2]), F32)
        out[each] = jnp.concatenate([end, rest], axis=0).astype(BF16)


def forward_kernel(counts, rows, cols, tiles, flat, total, sent, acc):
    slots, width = tiles.shape[2], tiles.shape[3]
    nrows, nprobe = total.shape[0], total.shape[1]
    acc[...] = jnp.zeros_like(acc)
    live = counts[0, 0]
    outs = []
    for group in groups(slots):
        left = jnp.concatenate([flat[cols[0, 0, n]] for n in group], axis=0)
        right = jnp.concatenate([tiles[0, 0, n] for n in group], axis=0)
        out = lax.dot_general(left, right, (((1,), (1,)), ((), ())), preferred_element_type=F32)
        outs += [
            (n, out[i * nprobe : (i + 1) * nprobe, i * width : (i + 1) * width])
            for i, n in enumerate(group)
        ]
    for n, out in outs:
        acc[jnp.where(n < live, rows[0, 0, n], nrows)] += out
    value = acc[0:nrows]
    total[...] = value
    sent[...] = value.astype(BF16)


def backward_kernel(
    counts, rows, cols, tiles, total, got, weight, probes, stiff, paired, odd, part, weighted, acc
):
    slots, width = tiles.shape[2], tiles.shape[3]
    nrows, nprobe = total.shape[0], total.shape[1]
    ncols = part.shape[0]
    for k in range(nrows):
        value = total[k] + got[k].astype(F32)
        weighted[k] = (value * weight[k : k + 1, :]).astype(BF16)
    acc[...] = jnp.zeros_like(acc)
    live = counts[0, 0]
    outs = []
    for group in groups(slots):
        left = jnp.concatenate([weighted[rows[0, 0, n]] for n in group], axis=0)
        right = jnp.concatenate([tiles[0, 0, n] for n in group], axis=1)
        out = jnp.dot(left, right, preferred_element_type=F32)
        outs += [
            (n, out[i * nprobe : (i + 1) * nprobe, i * width : (i + 1) * width])
            for i, n in enumerate(group)
        ]
    for n, out in outs:
        acc[jnp.where(n < live, cols[0, 0, n], ncols)] += out
    each = paired.shape[0] - 1
    slabs = ncols // each
    mine = lax.axis_index("ray") == 1
    even, cell = even_cell(), lax.axis_index("cell")
    inner = jnp.logical_and(cell > 0, cell < lax.axis_size("cell") - 1)
    for s, near in (
        (0, jnp.where(even, odd[...], paired[...]).astype(F32)),
        (slabs - 1, jnp.where(even, paired[...], odd[...]).astype(F32)),
    ):
        there = jnp.logical_or(inner, even if s else jnp.logical_not(even))
        near = jnp.where(there, near, 0.0)
        for j in range(each):
            row = j * slabs + s
            scale = 0.5 * (stiff[row : row + 1, :] + near[each, j : j + 1, :])
            term = scale * (probes[rows_of(probes, s, j, slabs, ncols), :] - near[j])
            acc[s * each + j] += jnp.where(mine, term, 0.0)
    part[...] = acc[0:ncols].astype(BF16)


def smooth_kernel(probes, stiff, smooth, each):
    ncols, nprobe, width = smooth.shape
    slabs = ncols // each
    lane = lax.broadcasted_iota(I32, (1, width), 1)
    at_z = lane % NZ

    def stiff_at(s, j):
        if j < 0 or j >= each:
            return jnp.zeros((1, width), F32)
        return stiff[j * slabs + s : j * slabs + s + 1, :]

    def probe_at(s, j):
        if j < 0 or j >= each:
            return jnp.zeros((nprobe, width), F32)
        return probes[rows_of(probes, s, j, slabs, ncols), :]

    def up(value, by):
        return pltpu.roll(value, width - by, 1)

    def down(value, by):
        return pltpu.roll(value, by, 1)

    def neighbours(at, s, j):
        here, before, after = at(s, j), at(s, j - 1), at(s, j + 1)
        return [at(t, j) for t in (s - 1, s + 1) if 0 <= t < slabs] + [
            jnp.where(lane < width - NZ, up(here, NZ), up(after, NZ)),
            jnp.where(lane >= NZ, down(here, NZ), down(before, NZ)),
            jnp.where(at_z < NZ - 1, up(here, 1), 0.0),
            jnp.where(at_z > 0, down(here, 1), 0.0),
        ]

    for s in range(slabs):
        for j in range(each):
            here_s, here_p = stiff_at(s, j), probe_at(s, j)
            term = jnp.zeros((nprobe, width), F32)
            for near_s, near_p in zip(neighbours(stiff_at, s, j), neighbours(probe_at, s, j)):
                term = term + 0.5 * (here_s + near_s) * (here_p - near_p)
            smooth[s * each + j] = term


def combine_kernel(probes, smooth, mine, other, applied, diag, each):
    ncols = smooth.shape[0]
    slabs = ncols // each
    for s in range(slabs):
        for j in range(each):
            c, row = s * each + j, j * slabs + s
            value = mine[c].astype(F32) + other[c].astype(F32) + smooth[c]
            span = rows_of(probes, s, j, slabs, ncols)
            applied[span, :] = value
            diag[row : row + 1, :] = jnp.mean(probes[span, :] * value, axis=0, keepdims=True)


def to_rows(value, width):
    *lead, slabs, plane = value.shape
    value = value.reshape(*lead, slabs, plane // width, width)
    return jnp.swapaxes(value, -2, -3).reshape(-1, width)


def from_rows(value, shape):
    *lead, slabs, plane = shape
    width = value.shape[1]
    value = value.reshape(*lead, plane // width, slabs, width)
    return jnp.swapaxes(value, -2, -3).reshape(shape)


def local(blocks, row_ids, col_ids, counts, ray_weight, probes, stiffness):
    slots, width = blocks.shape[2], blocks.shape[3]
    nprobe, slabs, plane = probes.shape
    ncols = slabs * plane // width
    nrows = ray_weight.shape[0] // width
    each = plane // width
    ncell, nray = lax.axis_size("cell"), lax.axis_size("ray")
    assert ncell > 1 and ncell & (ncell - 1) == 0 and nray == 2
    params = pltpu.CompilerParams(vmem_limit_bytes=8 * 1024 * 1024)

    def cost(flops, moved):
        return pl.CostEstimate(flops=flops, bytes_accessed=moved, transcendentals=0)

    products = cost(2 * slots * nprobe * width * width, 2 * slots * width * width)
    edge = pltpu.VMEM((each + 1, nprobe, width), BF16)
    pinned = [
        pltpu.with_memory_space_constraint(x, pltpu.HBM)
        for x in (row_ids, col_ids, to_rows(probes, width), to_rows(stiffness, width))
    ]
    flat, paired, odd, grid, stiff, rows, cols = pl.pallas_call(
        prepare_kernel,
        out_shape=(
            pltpu.VMEM((ncols, nprobe, width), BF16),
            edge,
            edge,
            pltpu.VMEM((nprobe * ncols, width), F32),
            pltpu.VMEM((ncols, width), F32),
            pltpu.SMEM(row_ids.shape, I32),
            pltpu.SMEM(col_ids.shape, I32),
        ),
        in_specs=[HBM] * 4,
        out_specs=(VMEM,) * 5 + (SMEM,) * 2,
        scratch_shapes=[pltpu.SemaphoreType.DMA((4,))],
        compiler_params=params,
        cost_estimate=cost(12 * 10**8, 1000),
        name="prepare",
    )(*pinned)

    total, sent = pl.pallas_call(
        forward_kernel,
        out_shape=(
            pltpu.VMEM((nrows, nprobe, width), F32),
            pltpu.VMEM((nrows, nprobe, width), BF16),
        ),
        in_specs=[SMEM] * 3 + [VMEM] * 2,
        out_specs=(VMEM,) * 2,
        scratch_shapes=[pltpu.VMEM((nrows + 1, nprobe, width), F32)],
        compiler_params=params,
        cost_estimate=products,
        name="forward",
    )(counts, rows, cols, blocks, flat)

    def swap(value, first, cores):
        ends = [(c * nray + r, (c + 1) * nray + r) for c in range(first, ncell - 1, 2) for r in cores]
        return lax.ppermute(value, ("cell", "ray"), ends + [(j, i) for i, j in ends])

    paired, odd = swap(paired, 0, (0, 1)), swap(odd, 1, (1,))

    steps = [1 << i for i in range(ncell.bit_length() - 1)]
    turns = list(zip(steps, steps[-1:] + steps[:-1]))
    for i, turn in enumerate(turns):
        pairs = [(c * nray + r, (c ^ turn[r]) * nray + r) for c in range(ncell) for r in range(nray)]
        got = lax.ppermute(sent, ("cell", "ray"), pairs)
        if i == 0:
            got, odd = lax.optimization_barrier((got, odd))
        if i < len(turns) - 1:
            total = total + got.astype(F32)
            sent = total.astype(BF16)
    got, paired = lax.optimization_barrier((got, paired))

    part = pl.pallas_call(
        backward_kernel,
        out_shape=pltpu.VMEM((ncols, nprobe, width), BF16),
        in_specs=[SMEM] * 3 + [VMEM] * 8,
        out_specs=VMEM,
        scratch_shapes=[
            pltpu.VMEM((nrows, nprobe, width), BF16),
            pltpu.VMEM((ncols + 1, nprobe, width), F32),
        ],
        compiler_params=params,
        cost_estimate=products,
        name="backward",
    )(counts, rows, cols, blocks, total, got, ray_weight.reshape(nrows, width), grid, stiff, paired, odd)

    other = lax.ppermute(part, "ray", [(0, 1), (1, 0)])

    smooth = pl.pallas_call(
        lambda *refs: smooth_kernel(*refs, each=each),
        out_shape=pltpu.VMEM((ncols, nprobe, width), F32),
        in_specs=[VMEM] * 2,
        out_specs=VMEM,
        compiler_params=params,
        name="smooth",
    )(grid, stiff)

    applied, diag = pl.pallas_call(
        lambda *refs: combine_kernel(*refs, each=each),
        out_shape=(
            jax.ShapeDtypeStruct((nprobe * ncols, width), F32),
            jax.ShapeDtypeStruct((ncols, width), F32),
        ),
        in_specs=[VMEM] * 4,
        out_specs=(VMEM, VMEM),
        compiler_params=params,
        name="combine",
    )(grid, smooth, part, other)
    return from_rows(applied, probes.shape), from_rows(diag, stiffness.shape)


def solution(mesh):
    return jax.shard_map(
        local,
        mesh=mesh,
        in_specs=(
            P(("region", "cell"), "ray", None, None, None),
            P(("region", "cell"), "ray", None),
            P(("region", "cell"), "ray", None),
            P(("region", "cell"), "ray"),
            P(("region", "ray")),
            P(None, ("region", "cell"), None),
            P(("region", "cell"), None),
        ),
        out_specs=(P(None, ("region", "cell"), None), P(("region", "cell"), None)),
        check_vma=False,
    )
```

```python
import jax
import jax.numpy as jnp
from jax import lax
from jax.experimental import pallas as pl
from jax.experimental.pallas import tpu as pltpu
from jax.sharding import PartitionSpec as P

NZ = 32
F32 = jnp.float32
BF16 = jnp.bfloat16
I32 = jnp.int32
VMEM = pl.BlockSpec(memory_space=pltpu.VMEM)
SMEM = pl.BlockSpec(memory_space=pltpu.SMEM)
HBM = pl.BlockSpec(memory_space=pltpu.HBM)


def rows_of(ref, s, j, slabs, ncols):
    return pl.ds(j * slabs + s, ref.shape[0] // ncols, stride=ncols)


def groups(slots):
    return [tuple(range(n, min(n + 2, slots))) for n in range(0, slots, 2)]


def even_cell():
    return lax.rem(lax.axis_index("cell"), 2) == 0


def prepare_kernel(
    rows_in, cols_in, probes_in, stiff_in, flat, paired, odd, probes, stiff, rows, cols, sems
):
    ncols, slabs = flat.shape[0], stiff.shape[0] // (paired.shape[0] - 1)
    each = ncols // slabs
    pairs = [(probes_in, probes), (stiff_in, stiff), (rows_in, rows), (cols_in, cols)]
    copies = [pltpu.make_async_copy(a, b, sems.at[i]) for i, (a, b) in enumerate(pairs)]
    for copy in copies:
        copy.start()
    for copy in copies:
        copy.wait()
    for s in range(slabs):
        for j in range(each):
            flat[s * each + j] = probes[rows_of(probes, s, j, slabs, ncols), :].astype(BF16)
    even, top = even_cell(), (slabs - 1) * each
    for out, high in ((paired, even), (odd, jnp.logical_not(even))):
        for j in range(each):
            out[j] = jnp.where(high, flat[top + j], flat[j])
        low_end = stiff[pl.ds(0, each, stride=slabs), :]
        high_end = stiff[pl.ds(slabs - 1, each, stride=slabs), :]
        end = jnp.where(high, high_end, low_end)
        rest = jnp.zeros((out.shape[1] - each, out.shape[2]), F32)
        out[each] = jnp.concatenate([end, rest], axis=0).astype(BF16)


def forward_kernel(counts, rows, cols, tiles, flat, total, sent, acc):
    slots, width = tiles.shape[2], tiles.shape[3]
    nrows, nprobe = total.shape[0], total.shape[1]
    acc[...] = jnp.zeros_like(acc)
    live = counts[0, 0]
    outs = []
    for group in groups(slots):
        left = jnp.concatenate([flat[cols[0, 0, n]] for n in group], axis=0)
        right = jnp.concatenate([tiles[0, 0, n].T for n in group], axis=1)
        out = jnp.dot(left, right, preferred_element_type=F32)
        for i, n in enumerate(group):
            acc[jnp.where(n < live, rows[0, 0, n], nrows)] += out[i * nprobe : (i + 1) * nprobe, i * width : (i + 1) * width]
    value = acc[0:nrows]
    total[...] = value
    sent[...] = value.astype(BF16)


def backward_kernel(
    counts, rows, cols, tiles, total, got, weight, probes, stiff, odd, part, weighted, acc
):
    slots, width = tiles.shape[2], tiles.shape[3]
    nrows, nprobe = total.shape[0], total.shape[1]
    ncols = part.shape[0]
    for k in range(nrows):
        value = total[k] + got[k].astype(F32)
        weighted[k] = (value * weight[k : k + 1, :]).astype(BF16)
    acc[...] = jnp.zeros_like(acc)
    live = counts[0, 0]
    outs = []
    for group in groups(slots):
        left = jnp.concatenate([weighted[rows[0, 0, n]] for n in group], axis=0)
        right = jnp.concatenate([tiles[0, 0, n] for n in group], axis=1)
        out = jnp.dot(left, right, preferred_element_type=F32)
        outs += [
            (n, out[i * nprobe : (i + 1) * nprobe, i * width : (i + 1) * width])
            for i, n in enumerate(group)
        ]
    for n, out in outs:
        acc[jnp.where(n < live, cols[0, 0, n], ncols)] += out
    each = odd.shape[0] - 1
    slabs = ncols // each
    even, cell = even_cell(), lax.axis_index("cell")
    inner = jnp.logical_and(cell > 0, cell < lax.axis_size("cell") - 1)
    mine = lax.axis_index("ray") == 1
    for s, here in ((0, even), (slabs - 1, jnp.logical_not(even))):
        for j in range(each):
            row = j * slabs + s
            scale = 0.5 * (stiff[row : row + 1, :] + jnp.where(inner, odd[each, j : j + 1, :].astype(F32), 0.0))
            near = jnp.where(inner, odd[j].astype(F32), 0.0)
            term = scale * (probes[rows_of(probes, s, j, slabs, ncols), :] - near)
            acc[s * each + j] += jnp.where(jnp.logical_and(mine, here), term, 0.0)
    part[...] = acc[0:ncols].astype(BF16)


def smooth_kernel(probes, stiff, paired, smooth, each):
    ncols, nprobe, width = smooth.shape
    slabs = ncols // each
    lane = lax.broadcasted_iota(I32, (1, width), 1)
    at_z = lane % NZ

    def stiff_at(s, j):
        if j < 0 or j >= each:
            return jnp.zeros((1, width), F32)
        return stiff[j * slabs + s : j * slabs + s + 1, :]

    def probe_at(s, j):
        if j < 0 or j >= each:
            return jnp.zeros((nprobe, width), F32)
        return probes[rows_of(probes, s, j, slabs, ncols), :]

    def up(value, by):
        return pltpu.roll(value, width - by, 1)

    def down(value, by):
        return pltpu.roll(value, by, 1)

    def neighbours(at, s, j):
        here, before, after = at(s, j), at(s, j - 1), at(s, j + 1)
        return [at(t, j) for t in (s - 1, s + 1) if 0 <= t < slabs] + [
            jnp.where(lane < width - NZ, up(here, NZ), up(after, NZ)),
            jnp.where(lane >= NZ, down(here, NZ), down(before, NZ)),
            jnp.where(at_z < NZ - 1, up(here, 1), 0.0),
            jnp.where(at_z > 0, down(here, 1), 0.0),
        ]

    for s in range(slabs):
        for j in range(each):
            here_s, here_p = stiff_at(s, j), probe_at(s, j)
            term = jnp.zeros((nprobe, width), F32)
            for near_s, near_p in zip(neighbours(stiff_at, s, j), neighbours(probe_at, s, j)):
                term = term + 0.5 * (here_s + near_s) * (here_p - near_p)
            smooth[s * each + j] = term
    even = even_cell()
    for s, here in ((0, jnp.logical_not(even)), (slabs - 1, even)):
        for j in range(each):
            scale = 0.5 * (stiff_at(s, j) + paired[each, j : j + 1, :].astype(F32))
            term = scale * (probe_at(s, j) - paired[j].astype(F32))
            smooth[s * each + j] += jnp.where(here, term, 0.0)


def combine_kernel(probes, smooth, mine, other, applied, diag, each):
    ncols = smooth.shape[0]
    slabs = ncols // each
    for s in range(slabs):
        for j in range(each):
            c, row = s * each + j, j * slabs + s
            value = mine[c].astype(F32) + other[c].astype(F32) + smooth[c]
            span = rows_of(probes, s, j, slabs, ncols)
            applied[span, :] = value
            diag[row : row + 1, :] = jnp.mean(probes[span, :] * value, axis=0, keepdims=True)


def to_rows(value, width):
    *lead, slabs, plane = value.shape
    value = value.reshape(*lead, slabs, plane // width, width)
    return jnp.swapaxes(value, -2, -3).reshape(-1, width)


def from_rows(value, shape):
    *lead, slabs, plane = shape
    width = value.shape[1]
    value = value.reshape(*lead, plane // width, slabs, width)
    return jnp.swapaxes(value, -2, -3).reshape(shape)


def local(blocks, row_ids, col_ids, counts, ray_weight, probes, stiffness):
    slots, width = blocks.shape[2], blocks.shape[3]
    nprobe, slabs, plane = probes.shape
    ncols = slabs * plane // width
    nrows = ray_weight.shape[0] // width
    each = plane // width
    ncell, nray = lax.axis_size("cell"), lax.axis_size("ray")
    assert ncell > 1 and ncell & (ncell - 1) == 0 and nray == 2
    params = pltpu.CompilerParams(vmem_limit_bytes=8 * 1024 * 1024)

    def cost(flops, moved):
        return pl.CostEstimate(flops=flops, bytes_accessed=moved, transcendentals=0)

    products = cost(2 * slots * nprobe * width * width, 2 * slots * width * width)
    edge = pltpu.VMEM((each + 1, nprobe, width), BF16)
    pinned = [
        pltpu.with_memory_space_constraint(x, pltpu.HBM)
        for x in (row_ids, col_ids, to_rows(probes, width), to_rows(stiffness, width))
    ]
    flat, paired, odd, grid, stiff, rows, cols = pl.pallas_call(
        prepare_kernel,
        out_shape=(
            pltpu.VMEM((ncols, nprobe, width), BF16),
            edge,
            edge,
            pltpu.VMEM((nprobe * ncols, width), F32),
            pltpu.VMEM((ncols, width), F32),
            pltpu.SMEM(row_ids.shape, I32),
            pltpu.SMEM(col_ids.shape, I32),
        ),
        in_specs=[HBM] * 4,
        out_specs=(VMEM,) * 5 + (SMEM,) * 2,
        scratch_shapes=[pltpu.SemaphoreType.DMA((4,))],
        compiler_params=params,
        cost_estimate=cost(12 * 10**8, 1000),
        name="prepare",
    )(*pinned)

    total, sent = pl.pallas_call(
        forward_kernel,
        out_shape=(
            pltpu.VMEM((nrows, nprobe, width), F32),
            pltpu.VMEM((nrows, nprobe, width), BF16),
        ),
        in_specs=[SMEM] * 3 + [VMEM] * 2,
        out_specs=(VMEM,) * 2,
        scratch_shapes=[pltpu.VMEM((nrows + 1, nprobe, width), F32)],
        compiler_params=params,
        cost_estimate=products,
        name="forward",
    )(counts, rows, cols, blocks, flat)

    def swap(value, first, cores):
        ends = [(c * nray + r, (c + 1) * nray + r) for c in range(first, ncell - 1, 2) for r in cores]
        return lax.ppermute(value, ("cell", "ray"), ends + [(j, i) for i, j in ends])

    paired, odd = swap(paired, 0, (0, 1)), swap(odd, 1, (1,))

    steps = [1 << i for i in range(ncell.bit_length() - 1)]
    turns = list(zip(steps, steps[-1:] + steps[:-1]))
    for i, turn in enumerate(turns):
        pairs = [(c * nray + r, (c ^ turn[r]) * nray + r) for c in range(ncell) for r in range(nray)]
        got = lax.ppermute(sent, ("cell", "ray"), pairs)
        if i < len(turns) - 1:
            total = total + got.astype(F32)
            sent = total.astype(BF16)
            if i == 0:
                sent, odd = lax.optimization_barrier((sent, odd))

    part = pl.pallas_call(
        backward_kernel,
        out_shape=pltpu.VMEM((ncols, nprobe, width), BF16),
        in_specs=[SMEM] * 3 + [VMEM] * 7,
        out_specs=VMEM,
        scratch_shapes=[
            pltpu.VMEM((nrows, nprobe, width), BF16),
            pltpu.VMEM((ncols + 1, nprobe, width), F32),
        ],
        compiler_params=params,
        cost_estimate=products,
        name="backward",
    )(counts, rows, cols, blocks, total, got, ray_weight.reshape(nrows, width), grid, stiff, odd)

    part, paired = lax.optimization_barrier((part, paired))
    other = lax.ppermute(part, "ray", [(0, 1), (1, 0)])

    smooth = pl.pallas_call(
        lambda *refs: smooth_kernel(*refs, each=each),
        out_shape=pltpu.VMEM((ncols, nprobe, width), F32),
        in_specs=[VMEM] * 3,
        out_specs=VMEM,
        compiler_params=params,
        name="smooth",
    )(grid, stiff, paired)

    applied, diag = pl.pallas_call(
        lambda *refs: combine_kernel(*refs, each=each),
        out_shape=(
            jax.ShapeDtypeStruct((nprobe * ncols, width), F32),
            jax.ShapeDtypeStruct((ncols, width), F32),
        ),
        in_specs=[VMEM] * 4,
        out_specs=(VMEM, VMEM),
        compiler_params=params,
        name="combine",
    )(grid, smooth, part, other)
    return from_rows(applied, probes.shape), from_rows(diag, stiffness.shape)


def solution(mesh):
    return jax.shard_map(
        local,
        mesh=mesh,
        in_specs=(
            P(("region", "cell"), "ray", None, None, None),
            P(("region", "cell"), "ray", None),
            P(("region", "cell"), "ray", None),
            P(("region", "cell"), "ray"),
            P(("region", "ray")),
            P(None, ("region", "cell"), None),
            P(("region", "cell"), None),
        ),
        out_specs=(P(None, ("region", "cell"), None), P(("region", "cell"), None)),
        check_vma=False,
    )
```

```python
import jax
import jax.numpy as jnp
from jax import lax
from jax.experimental import pallas as pl
from jax.experimental.pallas import tpu as pltpu
from jax.sharding import PartitionSpec as P

NZ = 32
F32 = jnp.float32
BF16 = jnp.bfloat16
I32 = jnp.int32
VMEM = pl.BlockSpec(memory_space=pltpu.VMEM)
SMEM = pl.BlockSpec(memory_space=pltpu.SMEM)
HBM = pl.BlockSpec(memory_space=pltpu.HBM)


def rows_of(ref, s, j, slabs, ncols):
    return pl.ds(j * slabs + s, ref.shape[0] // ncols, stride=ncols)


def groups(slots):
    return [tuple(range(n, min(n + 2, slots))) for n in range(0, slots, 2)]


def even_cell():
    return lax.rem(lax.axis_index("cell"), 2) == 0


def prepare_kernel(
    rows_in, cols_in, probes_in, stiff_in, flat, paired, odd, probes, stiff, rows, cols, sems
):
    ncols, slabs = flat.shape[0], stiff.shape[0] // (paired.shape[0] - 1)
    each = ncols // slabs
    pairs = [(probes_in, probes), (stiff_in, stiff), (rows_in, rows), (cols_in, cols)]
    copies = [pltpu.make_async_copy(a, b, sems.at[i]) for i, (a, b) in enumerate(pairs)]
    for copy in copies:
        copy.start()
    for copy in copies:
        copy.wait()
    for s in range(slabs):
        for j in range(each):
            flat[s * each + j] = probes[rows_of(probes, s, j, slabs, ncols), :].astype(BF16)
    even, top = even_cell(), (slabs - 1) * each
    for out, high in ((paired, even), (odd, jnp.logical_not(even))):
        for j in range(each):
            out[j] = jnp.where(high, flat[top + j], flat[j])
        low_end = stiff[pl.ds(0, each, stride=slabs), :]
        high_end = stiff[pl.ds(slabs - 1, each, stride=slabs), :]
        end = jnp.where(high, high_end, low_end)
        rest = jnp.zeros((out.shape[1] - each, out.shape[2]), F32)
        out[each] = jnp.concatenate([end, rest], axis=0).astype(BF16)


def forward_kernel(counts, rows, cols, tiles, flat, total, sent, acc):
    slots, width = tiles.shape[2], tiles.shape[3]
    nrows, nprobe = total.shape[0], total.shape[1]
    acc[...] = jnp.zeros_like(acc)
    live = counts[0, 0]
    outs = []
    for group in groups(slots):
        left = jnp.concatenate([flat[cols[0, 0, n]] for n in group], axis=0)
        if group[0] // 2 % 3 == 0:
            right = jnp.concatenate([tiles[0, 0, n] for n in group], axis=0)
            out = lax.dot_general(left, right, (((1,), (1,)), ((), ())), preferred_element_type=F32)
        else:
            right = jnp.concatenate([tiles[0, 0, n].T for n in group], axis=1)
            out = jnp.dot(left, right, preferred_element_type=F32)
        for i, n in enumerate(group):
            piece = out[i * nprobe : (i + 1) * nprobe, i * width : (i + 1) * width]
            acc[i, jnp.where(n < live, rows[0, 0, n], nrows)] += piece
    value = acc[0, 0:nrows] + acc[1, 0:nrows]
    total[...] = value
    sent[...] = value.astype(BF16)


def backward_kernel(
    counts, rows, cols, tiles, total, got, weight, probes, stiff, odd, part, weighted, acc
):
    slots, width = tiles.shape[2], tiles.shape[3]
    nrows, nprobe = total.shape[0], total.shape[1]
    ncols = part.shape[0]
    for k in range(nrows):
        value = total[k] + got[k].astype(F32)
        weighted[k] = (value * weight[k : k + 1, :]).astype(BF16)
    acc[...] = jnp.zeros_like(acc)
    live = counts[0, 0]
    outs = []
    for group in groups(slots):
        left = jnp.concatenate([weighted[rows[0, 0, n]] for n in group], axis=0)
        right = jnp.concatenate([tiles[0, 0, n] for n in group], axis=1)
        out = jnp.dot(left, right, preferred_element_type=F32)
        outs += [
            (n, out[i * nprobe : (i + 1) * nprobe, i * width : (i + 1) * width])
            for i, n in enumerate(group)
        ]
    for n, out in outs:
        acc[n % 2, jnp.where(n < live, cols[0, 0, n], ncols)] += out
    each = odd.shape[0] - 1
    slabs = ncols // each
    even, cell = even_cell(), lax.axis_index("cell")
    inner = jnp.logical_and(cell > 0, cell < lax.axis_size("cell") - 1)
    mine = lax.axis_index("ray") == 1
    for s, here in ((0, even), (slabs - 1, jnp.logical_not(even))):
        for j in range(each):
            row = j * slabs + s
            scale = 0.5 * (stiff[row : row + 1, :] + jnp.where(inner, odd[each, j : j + 1, :].astype(F32), 0.0))
            near = jnp.where(inner, odd[j].astype(F32), 0.0)
            term = scale * (probes[rows_of(probes, s, j, slabs, ncols), :] - near)
            acc[0, s * each + j] += jnp.where(jnp.logical_and(mine, here), term, 0.0)
    part[...] = (acc[0, 0:ncols] + acc[1, 0:ncols]).astype(BF16)


def smooth_kernel(probes, stiff, paired, smooth, each):
    ncols, nprobe, width = smooth.shape
    slabs = ncols // each
    lane = lax.broadcasted_iota(I32, (1, width), 1)
    at_z = lane % NZ

    def stiff_at(s, j):
        if j < 0 or j >= each:
            return jnp.zeros((1, width), F32)
        return stiff[j * slabs + s : j * slabs + s + 1, :]

    def probe_at(s, j):
        if j < 0 or j >= each:
            return jnp.zeros((nprobe, width), F32)
        return probes[rows_of(probes, s, j, slabs, ncols), :]

    def up(value, by):
        return pltpu.roll(value, width - by, 1)

    def down(value, by):
        return pltpu.roll(value, by, 1)

    def neighbours(at, s, j):
        here, before, after = at(s, j), at(s, j - 1), at(s, j + 1)
        return [at(t, j) for t in (s - 1, s + 1) if 0 <= t < slabs] + [
            jnp.where(lane < width - NZ, up(here, NZ), up(after, NZ)),
            jnp.where(lane >= NZ, down(here, NZ), down(before, NZ)),
            jnp.where(at_z < NZ - 1, up(here, 1), 0.0),
            jnp.where(at_z > 0, down(here, 1), 0.0),
        ]

    for s in range(slabs):
        for j in range(each):
            here_s, here_p = stiff_at(s, j), probe_at(s, j)
            term = jnp.zeros((nprobe, width), F32)
            for near_s, near_p in zip(neighbours(stiff_at, s, j), neighbours(probe_at, s, j)):
                term = term + 0.5 * (here_s + near_s) * (here_p - near_p)
            smooth[s * each + j] = term
    even = even_cell()
    for s, here in ((0, jnp.logical_not(even)), (slabs - 1, even)):
        for j in range(each):
            scale = 0.5 * (stiff_at(s, j) + paired[each, j : j + 1, :].astype(F32))
            term = scale * (probe_at(s, j) - paired[j].astype(F32))
            smooth[s * each + j] += jnp.where(here, term, 0.0)


def combine_kernel(probes, smooth, mine, other, applied, diag, each):
    ncols = smooth.shape[0]
    slabs = ncols // each
    for s in range(slabs):
        for j in range(each):
            c, row = s * each + j, j * slabs + s
            value = mine[c].astype(F32) + other[c].astype(F32) + smooth[c]
            span = rows_of(probes, s, j, slabs, ncols)
            applied[span, :] = value
            diag[row : row + 1, :] = jnp.mean(probes[span, :] * value, axis=0, keepdims=True)


def to_rows(value, width):
    *lead, slabs, plane = value.shape
    value = value.reshape(*lead, slabs, plane // width, width)
    return jnp.swapaxes(value, -2, -3).reshape(-1, width)


def from_rows(value, shape):
    *lead, slabs, plane = shape
    width = value.shape[1]
    value = value.reshape(*lead, plane // width, slabs, width)
    return jnp.swapaxes(value, -2, -3).reshape(shape)


def local(blocks, row_ids, col_ids, counts, ray_weight, probes, stiffness):
    slots, width = blocks.shape[2], blocks.shape[3]
    nprobe, slabs, plane = probes.shape
    ncols = slabs * plane // width
    nrows = ray_weight.shape[0] // width
    each = plane // width
    ncell, nray = lax.axis_size("cell"), lax.axis_size("ray")
    assert ncell > 1 and ncell & (ncell - 1) == 0 and nray == 2
    params = pltpu.CompilerParams(vmem_limit_bytes=8 * 1024 * 1024)

    def cost(flops, moved):
        return pl.CostEstimate(flops=flops, bytes_accessed=moved, transcendentals=0)

    products = cost(2 * slots * nprobe * width * width, 2 * slots * width * width)
    edge = pltpu.VMEM((each + 1, nprobe, width), BF16)
    pinned = [
        pltpu.with_memory_space_constraint(x, pltpu.HBM)
        for x in (row_ids, col_ids, to_rows(probes, width), to_rows(stiffness, width))
    ]
    flat, paired, odd, grid, stiff, rows, cols = pl.pallas_call(
        prepare_kernel,
        out_shape=(
            pltpu.VMEM((ncols, nprobe, width), BF16),
            edge,
            edge,
            pltpu.VMEM((nprobe * ncols, width), F32),
            pltpu.VMEM((ncols, width), F32),
            pltpu.SMEM(row_ids.shape, I32),
            pltpu.SMEM(col_ids.shape, I32),
        ),
        in_specs=[HBM] * 4,
        out_specs=(VMEM,) * 5 + (SMEM,) * 2,
        scratch_shapes=[pltpu.SemaphoreType.DMA((4,))],
        compiler_params=params,
        cost_estimate=cost(12 * 10**8, 1000),
        name="prepare",
    )(*pinned)

    total, sent = pl.pallas_call(
        forward_kernel,
        out_shape=(
            pltpu.VMEM((nrows, nprobe, width), F32),
            pltpu.VMEM((nrows, nprobe, width), BF16),
        ),
        in_specs=[SMEM] * 3 + [VMEM] * 2,
        out_specs=(VMEM,) * 2,
        scratch_shapes=[pltpu.VMEM((2, nrows + 1, nprobe, width), F32)],
        compiler_params=params,
        cost_estimate=products,
        name="forward",
    )(counts, rows, cols, blocks, flat)

    def swap(value, first, cores):
        ends = [(c * nray + r, (c + 1) * nray + r) for c in range(first, ncell - 1, 2) for r in cores]
        return lax.ppermute(value, ("cell", "ray"), ends + [(j, i) for i, j in ends])

    paired, odd = swap(paired, 0, (0, 1)), swap(odd, 1, (1,))

    steps = [1 << i for i in range(ncell.bit_length() - 1)]
    turns = list(zip(steps, steps[-1:] + steps[:-1]))
    for i, turn in enumerate(turns):
        pairs = [(c * nray + r, (c ^ turn[r]) * nray + r) for c in range(ncell) for r in range(nray)]
        got = lax.ppermute(sent, ("cell", "ray"), pairs)
        if i < len(turns) - 1:
            total = total + got.astype(F32)
            sent = total.astype(BF16)
            if i == 0:
                sent, odd = lax.optimization_barrier((sent, odd))

    part = pl.pallas_call(
        backward_kernel,
        out_shape=pltpu.VMEM((ncols, nprobe, width), BF16),
        in_specs=[SMEM] * 3 + [VMEM] * 7,
        out_specs=VMEM,
        scratch_shapes=[
            pltpu.VMEM((nrows, nprobe, width), BF16),
            pltpu.VMEM((2, ncols + 1, nprobe, width), F32),
        ],
        compiler_params=params,
        cost_estimate=products,
        name="backward",
    )(counts, rows, cols, blocks, total, got, ray_weight.reshape(nrows, width), grid, stiff, odd)

    part, paired = lax.optimization_barrier((part, paired))
    other = lax.ppermute(part, "ray", [(0, 1), (1, 0)])

    smooth = pl.pallas_call(
        lambda *refs: smooth_kernel(*refs, each=each),
        out_shape=pltpu.VMEM((ncols, nprobe, width), F32),
        in_specs=[VMEM] * 3,
        out_specs=VMEM,
        compiler_params=params,
        name="smooth",
    )(grid, stiff, paired)

    applied, diag = pl.pallas_call(
        lambda *refs: combine_kernel(*refs, each=each),
        out_shape=(
            jax.ShapeDtypeStruct((nprobe * ncols, width), F32),
            jax.ShapeDtypeStruct((ncols, width), F32),
        ),
        in_specs=[VMEM] * 4,
        out_specs=(VMEM, VMEM),
        compiler_params=params,
        name="combine",
    )(grid, smooth, part, other)
    return from_rows(applied, probes.shape), from_rows(diag, stiffness.shape)


def solution(mesh):
    return jax.shard_map(
        local,
        mesh=mesh,
        in_specs=(
            P(("region", "cell"), "ray", None, None, None),
            P(("region", "cell"), "ray", None),
            P(("region", "cell"), "ray", None),
            P(("region", "cell"), "ray"),
            P(("region", "ray")),
            P(None, ("region", "cell"), None),
            P(("region", "cell"), None),
        ),
        out_specs=(P(None, ("region", "cell"), None), P(("region", "cell"), None)),
        check_vma=False,
    )
```

```python
import jax
import jax.numpy as jnp
from jax import lax
from jax.experimental import pallas as pl
from jax.experimental.pallas import tpu as pltpu
from jax.sharding import PartitionSpec as P

NZ = 32
F32 = jnp.float32
BF16 = jnp.bfloat16
I32 = jnp.int32
VMEM = pl.BlockSpec(memory_space=pltpu.VMEM)
SMEM = pl.BlockSpec(memory_space=pltpu.SMEM)
HBM = pl.BlockSpec(memory_space=pltpu.HBM)


def rows_of(ref, s, j, slabs, ncols):
    return pl.ds(j * slabs + s, ref.shape[0] // ncols, stride=ncols)


def groups(slots):
    return [tuple(range(n, min(n + 2, slots))) for n in range(0, slots, 2)]


def looks_up():
    return lax.rem(lax.axis_index("cell") + lax.axis_index("ray"), 2) == 0


def prepare_kernel(
    rows_in, cols_in, probes_in, stiff_in, flat, edge, probes, stiff, rows, cols, sems
):
    ncols, slabs = flat.shape[0], stiff.shape[0] // (edge.shape[0] - 1)
    each = ncols // slabs
    pairs = [(probes_in, probes), (stiff_in, stiff), (rows_in, rows), (cols_in, cols)]
    copies = [pltpu.make_async_copy(a, b, sems.at[i]) for i, (a, b) in enumerate(pairs)]
    for copy in copies:
        copy.start()
    for copy in copies:
        copy.wait()
    for s in range(slabs):
        for j in range(each):
            flat[s * each + j] = probes[rows_of(probes, s, j, slabs, ncols), :].astype(BF16)
    high, top = looks_up(), (slabs - 1) * each
    for j in range(each):
        edge[j] = jnp.where(high, flat[top + j], flat[j])
    low_end = stiff[pl.ds(0, each, stride=slabs), :]
    high_end = stiff[pl.ds(slabs - 1, each, stride=slabs), :]
    end = jnp.where(high, high_end, low_end)
    rest = jnp.zeros((edge.shape[1] - each, edge.shape[2]), F32)
    edge[each] = jnp.concatenate([end, rest], axis=0).astype(BF16)


def forward_kernel(counts, rows, cols, tiles, flat, total, sent, acc):
    slots, width = tiles.shape[2], tiles.shape[3]
    nrows, nprobe = total.shape[0], total.shape[1]
    acc[...] = jnp.zeros_like(acc)
    live = counts[0, 0]
    outs = []
    for group in groups(slots):
        left = jnp.concatenate([flat[cols[0, 0, n]] for n in group], axis=0)
        if group[0] // 2 % 3 == 0:
            right = jnp.concatenate([tiles[0, 0, n] for n in group], axis=0)
            out = lax.dot_general(left, right, (((1,), (1,)), ((), ())), preferred_element_type=F32)
        else:
            right = jnp.concatenate([tiles[0, 0, n].T for n in group], axis=1)
            out = jnp.dot(left, right, preferred_element_type=F32)
        for i, n in enumerate(group):
            piece = out[i * nprobe : (i + 1) * nprobe, i * width : (i + 1) * width]
            acc[i, jnp.where(n < live, rows[0, 0, n], nrows)] += piece
    value = acc[0, 0:nrows] + acc[1, 0:nrows]
    total[...] = value
    sent[...] = value.astype(BF16)


def backward_kernel(
    counts, rows, cols, tiles, total, got, weight, term, part, weighted, acc
):
    slots, width = tiles.shape[2], tiles.shape[3]
    nrows, nprobe = total.shape[0], total.shape[1]
    ncols = part.shape[0]
    for k in range(nrows):
        value = total[k] + got[k].astype(F32)
        weighted[k] = (value * weight[k : k + 1, :]).astype(BF16)
    acc[...] = jnp.zeros_like(acc)
    live = counts[0, 0]
    outs = []
    for group in groups(slots):
        left = jnp.concatenate([weighted[rows[0, 0, n]] for n in group], axis=0)
        right = jnp.concatenate([tiles[0, 0, n] for n in group], axis=1)
        out = jnp.dot(left, right, preferred_element_type=F32)
        outs += [
            (n, out[i * nprobe : (i + 1) * nprobe, i * width : (i + 1) * width])
            for i, n in enumerate(group)
        ]
    for n, out in outs:
        acc[n % 2, jnp.where(n < live, cols[0, 0, n], ncols)] += out
    half = term.shape[0] // 2
    acc[0, 0:half] += term[0:half]
    acc[0, ncols - half : ncols] += term[half:]
    part[...] = (acc[0, 0:ncols] + acc[1, 0:ncols]).astype(BF16)


def smooth_kernel(probes, stiff, beyond, smooth, term, each):
    ncols, nprobe, width = smooth.shape
    slabs = ncols // each
    lane = lax.broadcasted_iota(I32, (1, width), 1)
    at_z = lane % NZ

    def stiff_at(s, j):
        if j < 0 or j >= each:
            return jnp.zeros((1, width), F32)
        return stiff[j * slabs + s : j * slabs + s + 1, :]

    def probe_at(s, j):
        if j < 0 or j >= each:
            return jnp.zeros((nprobe, width), F32)
        return probes[rows_of(probes, s, j, slabs, ncols), :]

    def up(value, by):
        return pltpu.roll(value, width - by, 1)

    def down(value, by):
        return pltpu.roll(value, by, 1)

    def neighbours(at, s, j):
        here, before, after = at(s, j), at(s, j - 1), at(s, j + 1)
        return [at(t, j) for t in (s - 1, s + 1) if 0 <= t < slabs] + [
            jnp.where(lane < width - NZ, up(here, NZ), up(after, NZ)),
            jnp.where(lane >= NZ, down(here, NZ), down(before, NZ)),
            jnp.where(at_z < NZ - 1, up(here, 1), 0.0),
            jnp.where(at_z > 0, down(here, 1), 0.0),
        ]

    for s in range(slabs):
        for j in range(each):
            here_s, here_p = stiff_at(s, j), probe_at(s, j)
            value = jnp.zeros((nprobe, width), F32)
            for near_s, near_p in zip(neighbours(stiff_at, s, j), neighbours(probe_at, s, j)):
                value = value + 0.5 * (here_s + near_s) * (here_p - near_p)
            smooth[s * each + j] = value
    high, cell = looks_up(), lax.axis_index("cell")
    inner = jnp.logical_and(cell > 0, cell < lax.axis_size("cell") - 1)
    there = jnp.logical_or(inner, lax.axis_index("ray") == 0)
    for i, (s, here) in enumerate(((0, jnp.logical_not(high)), (slabs - 1, high))):
        for j in range(each):
            near_s = jnp.where(there, beyond[each, j : j + 1, :].astype(F32), 0.0)
            near_p = jnp.where(there, beyond[j].astype(F32), 0.0)
            value = 0.5 * (stiff_at(s, j) + near_s) * (probe_at(s, j) - near_p)
            term[i * each + j] = jnp.where(here, value, 0.0)


def combine_kernel(probes, smooth, mine, other, applied, diag, each):
    ncols = smooth.shape[0]
    slabs = ncols // each
    for s in range(slabs):
        for j in range(each):
            c, row = s * each + j, j * slabs + s
            value = mine[c].astype(F32) + other[c].astype(F32) + smooth[c]
            span = rows_of(probes, s, j, slabs, ncols)
            applied[span, :] = value
            diag[row : row + 1, :] = jnp.mean(probes[span, :] * value, axis=0, keepdims=True)


def to_rows(value, width):
    *lead, slabs, plane = value.shape
    value = value.reshape(*lead, slabs, plane // width, width)
    return jnp.swapaxes(value, -2, -3).reshape(-1, width)


def from_rows(value, shape):
    *lead, slabs, plane = shape
    width = value.shape[1]
    value = value.reshape(*lead, plane // width, slabs, width)
    return jnp.swapaxes(value, -2, -3).reshape(shape)


def local(blocks, row_ids, col_ids, counts, ray_weight, probes, stiffness):
    slots, width = blocks.shape[2], blocks.shape[3]
    nprobe, slabs, plane = probes.shape
    ncols = slabs * plane // width
    nrows = ray_weight.shape[0] // width
    each = plane // width
    ncell, nray = lax.axis_size("cell"), lax.axis_size("ray")
    assert ncell > 1 and ncell & (ncell - 1) == 0 and nray == 2
    params = pltpu.CompilerParams(vmem_limit_bytes=8 * 1024 * 1024)

    def cost(flops, moved):
        return pl.CostEstimate(flops=flops, bytes_accessed=moved, transcendentals=0)

    products = cost(2 * slots * nprobe * width * width, 2 * slots * width * width)
    pinned = [
        pltpu.with_memory_space_constraint(x, pltpu.HBM)
        for x in (row_ids, col_ids, to_rows(probes, width), to_rows(stiffness, width))
    ]
    flat, edge, grid, stiff, rows, cols = pl.pallas_call(
        prepare_kernel,
        out_shape=(
            pltpu.VMEM((ncols, nprobe, width), BF16),
            pltpu.VMEM((each + 1, nprobe, width), BF16),
            pltpu.VMEM((nprobe * ncols, width), F32),
            pltpu.VMEM((ncols, width), F32),
            pltpu.SMEM(row_ids.shape, I32),
            pltpu.SMEM(col_ids.shape, I32),
        ),
        in_specs=[HBM] * 4,
        out_specs=(VMEM,) * 4 + (SMEM,) * 2,
        scratch_shapes=[pltpu.SemaphoreType.DMA((4,))],
        compiler_params=params,
        cost_estimate=cost(12 * 10**8, 1000),
        name="prepare",
    )(*pinned)

    total, sent = pl.pallas_call(
        forward_kernel,
        out_shape=(
            pltpu.VMEM((nrows, nprobe, width), F32),
            pltpu.VMEM((nrows, nprobe, width), BF16),
        ),
        in_specs=[SMEM] * 3 + [VMEM] * 2,
        out_specs=(VMEM,) * 2,
        scratch_shapes=[pltpu.VMEM((2, nrows + 1, nprobe, width), F32)],
        compiler_params=params,
        cost_estimate=products,
        name="forward",
    )(counts, rows, cols, blocks, flat)

    ends = {c * nray: (c ^ 1) * nray for c in range(ncell)}
    ends |= {c * nray + 1: ((c + 1 if c % 2 else c - 1) % ncell) * nray + 1 for c in range(ncell)}
    beyond = lax.ppermute(edge, ("cell", "ray"), list(ends.items()))

    smooth, term = pl.pallas_call(
        lambda *refs: smooth_kernel(*refs, each=each),
        out_shape=(
            pltpu.VMEM((ncols, nprobe, width), F32),
            pltpu.VMEM((2 * each, nprobe, width), F32),
        ),
        in_specs=[VMEM] * 3,
        out_specs=(VMEM, VMEM),
        compiler_params=params,
        cost_estimate=cost(5 * 10**9, 1000),
        name="smooth",
    )(grid, stiff, beyond)

    steps = [1 << i for i in range(ncell.bit_length() - 1)]
    turns = list(zip(steps, steps[-1:] + steps[:-1]))
    for i, turn in enumerate(turns):
        pairs = [(c * nray + r, (c ^ turn[r]) * nray + r) for c in range(ncell) for r in range(nray)]
        got = lax.ppermute(sent, ("cell", "ray"), pairs)
        if i == 1:
            got, smooth, term = lax.optimization_barrier((got, smooth, term))
        if i < len(turns) - 1:
            total = total + got.astype(F32)
            sent = total.astype(BF16)

    part = pl.pallas_call(
        backward_kernel,
        out_shape=pltpu.VMEM((ncols, nprobe, width), BF16),
        in_specs=[SMEM] * 3 + [VMEM] * 5,
        out_specs=VMEM,
        scratch_shapes=[
            pltpu.VMEM((nrows, nprobe, width), BF16),
            pltpu.VMEM((2, ncols + 1, nprobe, width), F32),
        ],
        compiler_params=params,
        cost_estimate=products,
        name="backward",
    )(counts, rows, cols, blocks, total, got, ray_weight.reshape(nrows, width), term)

    other = lax.ppermute(part, "ray", [(0, 1), (1, 0)])

    applied, diag = pl.pallas_call(
        lambda *refs: combine_kernel(*refs, each=each),
        out_shape=(
            jax.ShapeDtypeStruct((nprobe * ncols, width), F32),
            jax.ShapeDtypeStruct((ncols, width), F32),
        ),
        in_specs=[VMEM] * 4,
        out_specs=(VMEM, VMEM),
        compiler_params=params,
        name="combine",
    )(grid, smooth, part, other)
    return from_rows(applied, probes.shape), from_rows(diag, stiffness.shape)


def solution(mesh):
    return jax.shard_map(
        local,
        mesh=mesh,
        in_specs=(
            P(("region", "cell"), "ray", None, None, None),
            P(("region", "cell"), "ray", None),
            P(("region", "cell"), "ray", None),
            P(("region", "cell"), "ray"),
            P(("region", "ray")),
            P(None, ("region", "cell"), None),
            P(("region", "cell"), None),
        ),
        out_specs=(P(None, ("region", "cell"), None), P(("region", "cell"), None)),
        check_vma=False,
    )
```

```python
import jax
import jax.numpy as jnp
from jax import lax
from jax.experimental import pallas as pl
from jax.experimental.pallas import tpu as pltpu
from jax.sharding import PartitionSpec as P

NZ = 32
F32 = jnp.float32
BF16 = jnp.bfloat16
I32 = jnp.int32
VMEM = pl.BlockSpec(memory_space=pltpu.VMEM)
SMEM = pl.BlockSpec(memory_space=pltpu.SMEM)
HBM = pl.BlockSpec(memory_space=pltpu.HBM)


def rows_of(ref, s, j, slabs, ncols):
    return pl.ds(j * slabs + s, ref.shape[0] // ncols, stride=ncols)


def groups(slots):
    return [tuple(range(n, min(n + 2, slots))) for n in range(0, slots, 2)]


def looks_up():
    return lax.rem(lax.axis_index("cell") + lax.axis_index("ray"), 2) == 0


def prepare_kernel(
    rows_in, cols_in, probes_in, stiff_in, flat, edge, probes, stiff, rows, cols, sems
):
    ncols, slabs = flat.shape[0], stiff.shape[0] // (edge.shape[0] - 1)
    each = ncols // slabs
    pairs = [(probes_in, probes), (stiff_in, stiff), (rows_in, rows), (cols_in, cols)]
    copies = [pltpu.make_async_copy(a, b, sems.at[i]) for i, (a, b) in enumerate(pairs)]
    for copy in copies:
        copy.start()
    for copy in copies:
        copy.wait()
    for s in range(slabs):
        for j in range(each):
            flat[s * each + j] = probes[rows_of(probes, s, j, slabs, ncols), :].astype(BF16)
    high, top = looks_up(), (slabs - 1) * each
    for j in range(each):
        edge[j] = jnp.where(high, flat[top + j], flat[j])
    low_end = stiff[pl.ds(0, each, stride=slabs), :]
    high_end = stiff[pl.ds(slabs - 1, each, stride=slabs), :]
    end = jnp.where(high, high_end, low_end)
    rest = jnp.zeros((edge.shape[1] - each, edge.shape[2]), F32)
    edge[each] = jnp.concatenate([end, rest], axis=0).astype(BF16)


def forward_kernel(counts, rows, cols, tiles, flat, total, sent, acc):
    slots, width = tiles.shape[2], tiles.shape[3]
    nrows, nprobe = total.shape[0], total.shape[1]
    acc[...] = jnp.zeros_like(acc)
    live = counts[0, 0]
    outs = []
    for group in groups(slots):
        left = jnp.concatenate([flat[cols[0, 0, n]] for n in group], axis=0)
        if group[0] // 2 % 3 == 0:
            right = jnp.concatenate([tiles[0, 0, n] for n in group], axis=0)
            out = lax.dot_general(left, right, (((1,), (1,)), ((), ())), preferred_element_type=F32)
        else:
            right = jnp.concatenate([tiles[0, 0, n].T for n in group], axis=1)
            out = jnp.dot(left, right, preferred_element_type=F32)
        for i, n in enumerate(group):
            piece = out[i * nprobe : (i + 1) * nprobe, i * width : (i + 1) * width]
            acc[i, jnp.where(n < live, rows[0, 0, n], nrows)] += piece
    value = acc[0, 0:nrows] + acc[1, 0:nrows]
    total[...] = value
    sent[...] = value.astype(BF16)


def backward_kernel(
    rows, target, tiles, total, got, weight, term, part, weighted, acc
):
    slots, width = tiles.shape[2], tiles.shape[3]
    nrows, nprobe = total.shape[0], total.shape[1]
    ncols = part.shape[0]
    for k in range(nrows):
        value = total[k] + got[k].astype(F32)
        weighted[k] = (value * weight[k : k + 1, :]).astype(BF16)
    acc[...] = jnp.zeros_like(acc)
    outs = []
    for group in groups(slots):
        left = jnp.concatenate([weighted[rows[0, 0, n]] for n in group], axis=0)
        right = jnp.concatenate([tiles[0, 0, n] for n in group], axis=1)
        out = jnp.dot(left, right, preferred_element_type=F32)
        outs += [
            (n, out[i * nprobe : (i + 1) * nprobe, i * width : (i + 1) * width])
            for i, n in enumerate(group)
        ]
    for n, out in outs:
        acc[n % 2, target[0, 0, n]] += out
    half = term.shape[0] // 2
    acc[0, 0:half] += term[0:half]
    acc[0, ncols - half : ncols] += term[half:]
    part[...] = (acc[0, 0:ncols] + acc[1, 0:ncols]).astype(BF16)


def smooth_kernel(counts, cols, probes, stiff, beyond, smooth, term, target, each):
    ncols, nprobe, width = smooth.shape
    slabs = ncols // each
    for n in range(cols.shape[2]):
        target[0, 0, n] = jnp.where(n < counts[0, 0], cols[0, 0, n], ncols)
    lane = lax.broadcasted_iota(I32, (1, width), 1)
    at_z = lane % NZ

    def stiff_at(s, j):
        if j < 0 or j >= each:
            return jnp.zeros((1, width), F32)
        return stiff[j * slabs + s : j * slabs + s + 1, :]

    def probe_at(s, j):
        if j < 0 or j >= each:
            return jnp.zeros((nprobe, width), F32)
        return probes[rows_of(probes, s, j, slabs, ncols), :]

    def up(value, by):
        return pltpu.roll(value, width - by, 1)

    def down(value, by):
        return pltpu.roll(value, by, 1)

    def neighbours(at, s, j):
        here, before, after = at(s, j), at(s, j - 1), at(s, j + 1)
        return [at(t, j) for t in (s - 1, s + 1) if 0 <= t < slabs] + [
            jnp.where(lane < width - NZ, up(here, NZ), up(after, NZ)),
            jnp.where(lane >= NZ, down(here, NZ), down(before, NZ)),
            jnp.where(at_z < NZ - 1, up(here, 1), 0.0),
            jnp.where(at_z > 0, down(here, 1), 0.0),
        ]

    for s in range(slabs):
        for j in range(each):
            here_s, here_p = stiff_at(s, j), probe_at(s, j)
            value = jnp.zeros((nprobe, width), F32)
            for near_s, near_p in zip(neighbours(stiff_at, s, j), neighbours(probe_at, s, j)):
                value = value + 0.5 * (here_s + near_s) * (here_p - near_p)
            smooth[s * each + j] = value
    high, cell = looks_up(), lax.axis_index("cell")
    inner = jnp.logical_and(cell > 0, cell < lax.axis_size("cell") - 1)
    there = jnp.logical_or(inner, lax.axis_index("ray") == 0)
    for i, (s, here) in enumerate(((0, jnp.logical_not(high)), (slabs - 1, high))):
        for j in range(each):
            near_s = jnp.where(there, beyond[each, j : j + 1, :].astype(F32), 0.0)
            near_p = jnp.where(there, beyond[j].astype(F32), 0.0)
            value = 0.5 * (stiff_at(s, j) + near_s) * (probe_at(s, j) - near_p)
            term[i * each + j] = jnp.where(here, value, 0.0)


def combine_kernel(probes, smooth, mine, other, applied, diag, each):
    ncols = smooth.shape[0]
    slabs = ncols // each
    for s in range(slabs):
        for j in range(each):
            c, row = s * each + j, j * slabs + s
            value = mine[c].astype(F32) + other[c].astype(F32) + smooth[c]
            span = rows_of(probes, s, j, slabs, ncols)
            applied[span, :] = value
            diag[row : row + 1, :] = jnp.mean(probes[span, :] * value, axis=0, keepdims=True)


def to_rows(value, width):
    *lead, slabs, plane = value.shape
    value = value.reshape(*lead, slabs, plane // width, width)
    return jnp.swapaxes(value, -2, -3).reshape(-1, width)


def from_rows(value, shape):
    *lead, slabs, plane = shape
    width = value.shape[1]
    value = value.reshape(*lead, plane // width, slabs, width)
    return jnp.swapaxes(value, -2, -3).reshape(shape)


def local(blocks, row_ids, col_ids, counts, ray_weight, probes, stiffness):
    slots, width = blocks.shape[2], blocks.shape[3]
    nprobe, slabs, plane = probes.shape
    ncols = slabs * plane // width
    nrows = ray_weight.shape[0] // width
    each = plane // width
    ncell, nray = lax.axis_size("cell"), lax.axis_size("ray")
    assert ncell > 1 and ncell & (ncell - 1) == 0 and nray == 2
    params = pltpu.CompilerParams(vmem_limit_bytes=8 * 1024 * 1024)

    def cost(flops, moved):
        return pl.CostEstimate(flops=flops, bytes_accessed=moved, transcendentals=0)

    products = cost(2 * slots * nprobe * width * width, 2 * slots * width * width)
    pinned = [
        pltpu.with_memory_space_constraint(x, pltpu.HBM)
        for x in (row_ids, col_ids, to_rows(probes, width), to_rows(stiffness, width))
    ]
    flat, edge, grid, stiff, rows, cols = pl.pallas_call(
        prepare_kernel,
        out_shape=(
            pltpu.VMEM((ncols, nprobe, width), BF16),
            pltpu.VMEM((each + 1, nprobe, width), BF16),
            pltpu.VMEM((nprobe * ncols, width), F32),
            pltpu.VMEM((ncols, width), F32),
            pltpu.SMEM(row_ids.shape, I32),
            pltpu.SMEM(col_ids.shape, I32),
        ),
        in_specs=[HBM] * 4,
        out_specs=(VMEM,) * 4 + (SMEM,) * 2,
        scratch_shapes=[pltpu.SemaphoreType.DMA((4,))],
        compiler_params=params,
        cost_estimate=cost(12 * 10**8, 1000),
        name="prepare",
    )(*pinned)

    total, sent = pl.pallas_call(
        forward_kernel,
        out_shape=(
            pltpu.VMEM((nrows, nprobe, width), F32),
            pltpu.VMEM((nrows, nprobe, width), BF16),
        ),
        in_specs=[SMEM] * 3 + [VMEM] * 2,
        out_specs=(VMEM,) * 2,
        scratch_shapes=[pltpu.VMEM((2, nrows + 1, nprobe, width), F32)],
        compiler_params=params,
        cost_estimate=products,
        name="forward",
    )(counts, rows, cols, blocks, flat)

    ends = {c * nray: (c ^ 1) * nray for c in range(ncell)}
    ends |= {c * nray + 1: ((c + 1 if c % 2 else c - 1) % ncell) * nray + 1 for c in range(ncell)}
    beyond = lax.ppermute(edge, ("cell", "ray"), list(ends.items()))

    smooth, term, target = pl.pallas_call(
        lambda *refs: smooth_kernel(*refs, each=each),
        out_shape=(
            pltpu.VMEM((ncols, nprobe, width), F32),
            pltpu.VMEM((2 * each, nprobe, width), F32),
            pltpu.SMEM(col_ids.shape, I32),
        ),
        in_specs=[SMEM] * 2 + [VMEM] * 3,
        out_specs=(VMEM, VMEM, SMEM),
        compiler_params=params,
        cost_estimate=cost(5 * 10**9, 1000),
        name="smooth",
    )(counts, cols, grid, stiff, beyond)

    steps = [1 << i for i in range(ncell.bit_length() - 1)]
    turns = list(zip(steps, steps[-1:] + steps[:-1]))
    for i, turn in enumerate(turns):
        pairs = [(c * nray + r, (c ^ turn[r]) * nray + r) for c in range(ncell) for r in range(nray)]
        got = lax.ppermute(sent, ("cell", "ray"), pairs)
        if i == 1:
            got, smooth, term = lax.optimization_barrier((got, smooth, term))
        if i < len(turns) - 1:
            total = total + got.astype(F32)
            sent = total.astype(BF16)

    part = pl.pallas_call(
        backward_kernel,
        out_shape=pltpu.VMEM((ncols, nprobe, width), BF16),
        in_specs=[SMEM] * 2 + [VMEM] * 5,
        out_specs=VMEM,
        scratch_shapes=[
            pltpu.VMEM((nrows, nprobe, width), BF16),
            pltpu.VMEM((2, ncols + 1, nprobe, width), F32),
        ],
        compiler_params=params,
        cost_estimate=products,
        name="backward",
    )(rows, target, blocks, total, got, ray_weight.reshape(nrows, width), term)

    other = lax.ppermute(part, "ray", [(0, 1), (1, 0)])

    applied, diag = pl.pallas_call(
        lambda *refs: combine_kernel(*refs, each=each),
        out_shape=(
            jax.ShapeDtypeStruct((nprobe * ncols, width), F32),
            jax.ShapeDtypeStruct((ncols, width), F32),
        ),
        in_specs=[VMEM] * 4,
        out_specs=(VMEM, VMEM),
        compiler_params=params,
        name="combine",
    )(grid, smooth, part, other)
    return from_rows(applied, probes.shape), from_rows(diag, stiffness.shape)


def solution(mesh):
    return jax.shard_map(
        local,
        mesh=mesh,
        in_specs=(
            P(("region", "cell"), "ray", None, None, None),
            P(("region", "cell"), "ray", None),
            P(("region", "cell"), "ray", None),
            P(("region", "cell"), "ray"),
            P(("region", "ray")),
            P(None, ("region", "cell"), None),
            P(("region", "cell"), None),
        ),
        out_specs=(P(None, ("region", "cell"), None), P(("region", "cell"), None)),
        check_vma=False,
    )
```

```python
import jax
import jax.numpy as jnp
from jax import lax
from jax.experimental import pallas as pl
from jax.experimental.pallas import tpu as pltpu
from jax.sharding import PartitionSpec as P

NZ = 32
F32 = jnp.float32
BF16 = jnp.bfloat16
I32 = jnp.int32
VMEM = pl.BlockSpec(memory_space=pltpu.VMEM)
SMEM = pl.BlockSpec(memory_space=pltpu.SMEM)
HBM = pl.BlockSpec(memory_space=pltpu.HBM)


def rows_of(ref, s, j, slabs, ncols):
    return pl.ds(j * slabs + s, ref.shape[0] // ncols, stride=ncols)


def groups(slots):
    return [tuple(range(n, min(n + 2, slots))) for n in range(0, slots, 2)]


def looks_up():
    return lax.rem(lax.axis_index("cell") + lax.axis_index("ray"), 2) == 0


def prepare_kernel(
    rows_in, cols_in, probes_in, stiff_in, flat, edge, probes, stiff, rows, cols, sems
):
    ncols, slabs = flat.shape[0], stiff.shape[0] // (edge.shape[0] - 1)
    each = ncols // slabs
    pairs = [(probes_in, probes), (stiff_in, stiff), (rows_in, rows), (cols_in, cols)]
    copies = [pltpu.make_async_copy(a, b, sems.at[i]) for i, (a, b) in enumerate(pairs)]
    for copy in copies:
        copy.start()
    for copy in copies:
        copy.wait()
    for s in range(slabs):
        for j in range(each):
            flat[s * each + j] = probes[rows_of(probes, s, j, slabs, ncols), :].astype(BF16)
    high, top = looks_up(), (slabs - 1) * each
    for j in range(each):
        edge[j] = jnp.where(high, flat[top + j], flat[j])
    low_end = stiff[pl.ds(0, each, stride=slabs), :]
    high_end = stiff[pl.ds(slabs - 1, each, stride=slabs), :]
    end = jnp.where(high, high_end, low_end)
    rest = jnp.zeros((edge.shape[1] - each, edge.shape[2]), F32)
    edge[each] = jnp.concatenate([end, rest], axis=0).astype(BF16)


def forward_kernel(counts, rows, cols, tiles, flat, total, sent, acc):
    slots, width = tiles.shape[2], tiles.shape[3]
    nrows, nprobe = total.shape[0], total.shape[1]
    acc[...] = jnp.zeros_like(acc)
    live = counts[0, 0]
    outs = []
    for group in groups(slots):
        left = jnp.concatenate([flat[cols[0, 0, n]] for n in group], axis=0)
        if group[0] // 2 % 3 == 0:
            right = jnp.concatenate([tiles[0, 0, n] for n in group], axis=0)
            out = lax.dot_general(left, right, (((1,), (1,)), ((), ())), preferred_element_type=F32)
        else:
            right = jnp.concatenate([tiles[0, 0, n].T for n in group], axis=1)
            out = jnp.dot(left, right, preferred_element_type=F32)
        for i, n in enumerate(group):
            piece = out[i * nprobe : (i + 1) * nprobe, i * width : (i + 1) * width]
            acc[i, jnp.where(n < live, rows[0, 0, n], nrows)] += piece
    value = acc[0, 0:nrows] + acc[1, 0:nrows]
    total[...] = value
    sent[...] = value.astype(BF16)


def backward_kernel(
    rows, target, tiles, total, got, weight, term, part, weighted, acc
):
    slots, width = tiles.shape[2], tiles.shape[3]
    nrows, nprobe = total.shape[0], total.shape[1]
    ncols = part.shape[0]
    value = total[...] + got[...].astype(F32)
    weighted[...] = (value * weight[...][:, None, :]).astype(BF16)
    acc[...] = jnp.zeros_like(acc)
    outs = []
    for group in groups(slots):
        left = jnp.concatenate([weighted[rows[0, 0, n]] for n in group], axis=0)
        right = jnp.concatenate([tiles[0, 0, n] for n in group], axis=1)
        out = jnp.dot(left, right, preferred_element_type=F32)
        outs += [
            (n, out[i * nprobe : (i + 1) * nprobe, i * width : (i + 1) * width])
            for i, n in enumerate(group)
        ]
    for n, out in outs:
        acc[n % 2, target[0, 0, n]] += out
    half = term.shape[0] // 2
    acc[0, 0:half] += term[0:half]
    acc[0, ncols - half : ncols] += term[half:]
    part[...] = (acc[0, 0:ncols] + acc[1, 0:ncols]).astype(BF16)


def smooth_kernel(counts, cols, probes, stiff, beyond, smooth, term, target, each):
    ncols, nprobe, width = smooth.shape
    slabs = ncols // each
    for n in range(cols.shape[2]):
        target[0, 0, n] = jnp.where(n < counts[0, 0], cols[0, 0, n], ncols)
    lane = lax.broadcasted_iota(I32, (1, width), 1)
    at_z = lane % NZ

    def stiff_at(s, j):
        if j < 0 or j >= each:
            return jnp.zeros((1, width), F32)
        return stiff[j * slabs + s : j * slabs + s + 1, :]

    def probe_at(s, j):
        if j < 0 or j >= each:
            return jnp.zeros((nprobe, width), F32)
        return probes[rows_of(probes, s, j, slabs, ncols), :]

    def up(value, by):
        return pltpu.roll(value, width - by, 1)

    def down(value, by):
        return pltpu.roll(value, by, 1)

    def neighbours(at, s, j):
        here, before, after = at(s, j), at(s, j - 1), at(s, j + 1)
        return [at(t, j) for t in (s - 1, s + 1) if 0 <= t < slabs] + [
            jnp.where(lane < width - NZ, up(here, NZ), up(after, NZ)),
            jnp.where(lane >= NZ, down(here, NZ), down(before, NZ)),
            jnp.where(at_z < NZ - 1, up(here, 1), 0.0),
            jnp.where(at_z > 0, down(here, 1), 0.0),
        ]

    for s in range(slabs):
        for j in range(each):
            here_s, here_p = stiff_at(s, j), probe_at(s, j)
            value = jnp.zeros((nprobe, width), F32)
            for near_s, near_p in zip(neighbours(stiff_at, s, j), neighbours(probe_at, s, j)):
                value = value + 0.5 * (here_s + near_s) * (here_p - near_p)
            smooth[s * each + j] = value
    high, cell = looks_up(), lax.axis_index("cell")
    inner = jnp.logical_and(cell > 0, cell < lax.axis_size("cell") - 1)
    there = jnp.logical_or(inner, lax.axis_index("ray") == 0)
    for i, (s, here) in enumerate(((0, jnp.logical_not(high)), (slabs - 1, high))):
        for j in range(each):
            near_s = jnp.where(there, beyond[each, j : j + 1, :].astype(F32), 0.0)
            near_p = jnp.where(there, beyond[j].astype(F32), 0.0)
            value = 0.5 * (stiff_at(s, j) + near_s) * (probe_at(s, j) - near_p)
            term[i * each + j] = jnp.where(here, value, 0.0)


def combine_kernel(probes, smooth, mine, other, applied, diag, each):
    ncols = smooth.shape[0]
    slabs = ncols // each
    for s in range(slabs):
        for j in range(each):
            c, row = s * each + j, j * slabs + s
            value = mine[c].astype(F32) + other[c].astype(F32) + smooth[c]
            span = rows_of(probes, s, j, slabs, ncols)
            applied[span, :] = value
            diag[row : row + 1, :] = jnp.mean(probes[span, :] * value, axis=0, keepdims=True)


def to_rows(value, width):
    *lead, slabs, plane = value.shape
    value = value.reshape(*lead, slabs, plane // width, width)
    return jnp.swapaxes(value, -2, -3).reshape(-1, width)


def from_rows(value, shape):
    *lead, slabs, plane = shape
    width = value.shape[1]
    value = value.reshape(*lead, plane // width, slabs, width)
    return jnp.swapaxes(value, -2, -3).reshape(shape)


def local(blocks, row_ids, col_ids, counts, ray_weight, probes, stiffness):
    slots, width = blocks.shape[2], blocks.shape[3]
    nprobe, slabs, plane = probes.shape
    ncols = slabs * plane // width
    nrows = ray_weight.shape[0] // width
    each = plane // width
    ncell, nray = lax.axis_size("cell"), lax.axis_size("ray")
    assert ncell > 1 and ncell & (ncell - 1) == 0 and nray == 2
    params = pltpu.CompilerParams(vmem_limit_bytes=8 * 1024 * 1024)

    def cost(flops, moved):
        return pl.CostEstimate(flops=flops, bytes_accessed=moved, transcendentals=0)

    products = cost(2 * slots * nprobe * width * width, 2 * slots * width * width)
    pinned = [
        pltpu.with_memory_space_constraint(x, pltpu.HBM)
        for x in (row_ids, col_ids, to_rows(probes, width), to_rows(stiffness, width))
    ]
    flat, edge, grid, stiff, rows, cols = pl.pallas_call(
        prepare_kernel,
        out_shape=(
            pltpu.VMEM((ncols, nprobe, width), BF16),
            pltpu.VMEM((each + 1, nprobe, width), BF16),
            pltpu.VMEM((nprobe * ncols, width), F32),
            pltpu.VMEM((ncols, width), F32),
            pltpu.SMEM(row_ids.shape, I32),
            pltpu.SMEM(col_ids.shape, I32),
        ),
        in_specs=[HBM] * 4,
        out_specs=(VMEM,) * 4 + (SMEM,) * 2,
        scratch_shapes=[pltpu.SemaphoreType.DMA((4,))],
        compiler_params=params,
        cost_estimate=cost(12 * 10**8, 1000),
        name="prepare",
    )(*pinned)

    total, sent = pl.pallas_call(
        forward_kernel,
        out_shape=(
            pltpu.VMEM((nrows, nprobe, width), F32),
            pltpu.VMEM((nrows, nprobe, width), BF16),
        ),
        in_specs=[SMEM] * 3 + [VMEM] * 2,
        out_specs=(VMEM,) * 2,
        scratch_shapes=[pltpu.VMEM((2, nrows + 1, nprobe, width), F32)],
        compiler_params=params,
        cost_estimate=products,
        name="forward",
    )(counts, rows, cols, blocks, flat)

    ends = {c * nray: (c ^ 1) * nray for c in range(ncell)}
    ends |= {c * nray + 1: ((c + 1 if c % 2 else c - 1) % ncell) * nray + 1 for c in range(ncell)}
    beyond = lax.ppermute(edge, ("cell", "ray"), list(ends.items()))

    smooth, term, target = pl.pallas_call(
        lambda *refs: smooth_kernel(*refs, each=each),
        out_shape=(
            pltpu.VMEM((ncols, nprobe, width), F32),
            pltpu.VMEM((2 * each, nprobe, width), F32),
            pltpu.SMEM(col_ids.shape, I32),
        ),
        in_specs=[SMEM] * 2 + [VMEM] * 3,
        out_specs=(VMEM, VMEM, SMEM),
        compiler_params=params,
        cost_estimate=cost(5 * 10**9, 1000),
        name="smooth",
    )(counts, cols, grid, stiff, beyond)

    steps = [1 << i for i in range(ncell.bit_length() - 1)]
    turns = list(zip(steps, steps[-1:] + steps[:-1]))
    for i, turn in enumerate(turns):
        pairs = [(c * nray + r, (c ^ turn[r]) * nray + r) for c in range(ncell) for r in range(nray)]
        got = lax.ppermute(sent, ("cell", "ray"), pairs)
        if i == 1:
            got, smooth, term = lax.optimization_barrier((got, smooth, term))
        if i < len(turns) - 1:
            total = total + got.astype(F32)
            sent = total.astype(BF16)

    part = pl.pallas_call(
        backward_kernel,
        out_shape=pltpu.VMEM((ncols, nprobe, width), BF16),
        in_specs=[SMEM] * 2 + [VMEM] * 5,
        out_specs=VMEM,
        scratch_shapes=[
            pltpu.VMEM((nrows, nprobe, width), BF16),
            pltpu.VMEM((2, ncols + 1, nprobe, width), F32),
        ],
        compiler_params=params,
        cost_estimate=products,
        name="backward",
    )(rows, target, blocks, total, got, ray_weight.reshape(nrows, width), term)

    other = lax.ppermute(part, "ray", [(0, 1), (1, 0)])

    applied, diag = pl.pallas_call(
        lambda *refs: combine_kernel(*refs, each=each),
        out_shape=(
            jax.ShapeDtypeStruct((nprobe * ncols, width), F32),
            jax.ShapeDtypeStruct((ncols, width), F32),
        ),
        in_specs=[VMEM] * 4,
        out_specs=(VMEM, VMEM),
        compiler_params=params,
        name="combine",
    )(grid, smooth, part, other)
    return from_rows(applied, probes.shape), from_rows(diag, stiffness.shape)


def solution(mesh):
    return jax.shard_map(
        local,
        mesh=mesh,
        in_specs=(
            P(("region", "cell"), "ray", None, None, None),
            P(("region", "cell"), "ray", None),
            P(("region", "cell"), "ray", None),
            P(("region", "cell"), "ray"),
            P(("region", "ray")),
            P(None, ("region", "cell"), None),
            P(("region", "cell"), None),
        ),
        out_specs=(P(None, ("region", "cell"), None), P(("region", "cell"), None)),
        check_vma=False,
    )
```
